32 devices in a mesh: pipe: 2 (over core), seq: 4 (over y, x), dp: 4 (over z).
Axes of the slice: x: 2, y: 2, z: 4, core: 2. Of those that a mesh axis runs over, the one named last changes fastest.
Arguments:
- encoded: bfloat16 [4, 256, 4096], P('dp', 'seq'), may hold values from -6 to 6
- sent_forward: bfloat16 [2, 4, 256, 4096], P('pipe', 'dp', 'seq'), may hold values from -6 to 6
- head_cotangent: bfloat16 [4, 256, 4096], P('dp', 'seq'), may hold values from -6 to 6
- grad_sent: bfloat16 [2, 4, 256, 4096], P('pipe', 'dp', 'seq'), may hold values from -6 to 6
- x_saved: bfloat16 [2, 4, 256, 4096], P('pipe', 'dp', 'seq'), may hold values from -6 to 6
- q_saved: bfloat16 [2, 4, 256, 2048], P('pipe', 'dp', None, 'seq'), may hold values from -6 to 6
- k_saved: bfloat16 [2, 4, 256, 2048], P('pipe', 'dp', None, 'seq'), may hold values from -6 to 6
- v_saved: bfloat16 [2, 4, 256, 2048], P('pipe', 'dp', None, 'seq'), may hold values from -6 to 6
- norm_gain: float32 [2, 4096], P('pipe'), may hold values from 0.25 to 1.75
- logit_scale: float32 [2, 16], P('pipe', 'seq'), may hold values from 0.25 to 48
- w_query: bfloat16 [2, 4096, 2048], P('pipe', None, 'seq'), may hold values from -0.09375 to 0.09375
- w_key: bfloat16 [2, 4096, 2048], P('pipe', None, 'seq'), may hold values from -0.09375 to 0.09375
- w_value: bfloat16 [2, 4096, 2048], P('pipe', None, 'seq'), may hold values from -0.09375 to 0.09375
- w_out: bfloat16 [2, 2048, 4096], P('pipe', 'seq'), may hold values from -0.5 to 0.5
- key_blocks: int32 [4, 2, 2], P('dp'), may hold values from 0 to 1, as said below
- key_counts: int32 [4, 2], P('dp'), may hold values from 1 to 2, as said below
Outputs:
- forward_out: bfloat16 [2, 4, 256, 4096], P('pipe', 'dp', 'seq')
- back_out: bfloat16 [2, 4, 256, 4096], P('pipe', 'dp', 'seq')
- grad_query: bfloat16 [2, 4096, 2048], P('pipe', 'dp', 'seq')
- grad_key: bfloat16 [2, 4096, 2048], P('pipe', 'dp', 'seq')
- grad_value: bfloat16 [2, 4096, 2048], P('pipe', 'dp', 'seq')
- grad_out_proj: bfloat16 [2, 2048, 4096], P('pipe', 'seq', 'dp')
- grad_gain: float32 [2, 4096], P('pipe')
The draws below stay inside these ranges and needn't reach their ends.
Inputs may be any that keep to these rules, and one draw needn't show every extreme that they name: `key_blocks`: for each sample and query block i, the first key_counts entries of its list are different block numbers and the first is i itself; entries after them are block numbers that are not used. `key_counts`: in every sample some query block uses all 2 slots.
All inputs are finite; a program needn't handle non-finite values.
Results may differ from the reference program's by a relative error of at most 0.025.
The reference program's roundings to bfloat16 on the way (of `attended`, `saved_attended`, `grad_attended` and `grad_scores`) count: a program that leaves them out, or rounds other values in their place, can miss the bound.
Values may be sent and summed in bfloat16 or wider, within the bound.
No kernel may reach another device: no remote copies, remote signals or barrier semaphores. Data moves between devices by JAX's collectives and lax.ppermute only.
A program may use at most 128 MiB of HBM per device.

```python
import math
import jax
import jax.numpy as jnp
from jax import lax

D = 4096
HEADS = 16
HD = 128
BLOCK = 128
SECTIONS = 2
SAMPLES = 4
SEQ = 256
NBLK = 2
KMAX = 2
N_SEQ = 4


def pattern_draw(key):
    order_key, count_key, pick_key = jax.random.split(key, 3)
    row_keys = jax.random.split(order_key, SAMPLES * NBLK)
    orders = jax.vmap(lambda row_key: jax.random.permutation(row_key, NBLK))(row_keys)
    orders = orders.reshape(SAMPLES, NBLK, NBLK).astype(jnp.int32)
    own_block = jnp.arange(NBLK, dtype=jnp.int32)[None, :, None]
    leading = orders[:, :, :1]
    swapped = jnp.where(orders == own_block, leading, orders)
    swapped = jnp.concatenate([jnp.broadcast_to(own_block, (SAMPLES, NBLK, 1)), swapped[:, :, 1:]], axis=2)
    block_ids = swapped[:, :, :KMAX].astype(jnp.int32)
    counts = jax.random.randint(count_key, (SAMPLES, NBLK), 1, KMAX + 1).astype(jnp.int32)
    full_row = jax.random.randint(pick_key, (SAMPLES,), 0, NBLK).astype(jnp.int32)
    positions = jnp.arange(NBLK, dtype=jnp.int32)[None, :]
    counts = jnp.where(positions == full_row[:, None], KMAX, counts).astype(jnp.int32)
    return (block_ids, counts)


def draw_key_blocks(key, part):
    shared = pattern_draw(key)
    return shared[0]


def draw_key_counts(key, part):
    shared = pattern_draw(key)
    return shared[1]


def draw_logit_scale(key, part):
    key = jax.random.fold_in(key, 5)
    lowest, highest = (0.25, 4.0)
    spread = jax.random.uniform(key, (SECTIONS, HEADS), jnp.float32)
    return jnp.exp(jnp.log(lowest) + spread * (jnp.log(highest) - jnp.log(lowest))).astype(jnp.float32)


def steps_of(key, dims, cuts, low, high):
    factor_of, own = 1.0, jax.random.fold_in(key, 6)
    for dim, parts in cuts:
        draws = jnp.exp(jax.random.uniform(jax.random.fold_in(own, dim), (parts,), jnp.float32, low / len(cuts), high / len(cuts)))
        factor_of = factor_of * jnp.repeat(draws, dims[dim] // parts).reshape([-1 if axis == dim else 1 for axis in range(len(dims))])
    return factor_of


def normal_values(stream_key, extent, scale, reach, pieces=(), held_as=jnp.bfloat16):
    loudness = steps_of(stream_key, extent, pieces, -0.22, 0.18) if pieces else 1.0
    result = jax.random.normal(stream_key, extent, jnp.float32) * scale * loudness
    return jnp.minimum(jnp.maximum(result, -reach), reach).astype(held_as)


def setup_inputs(seed: int = 0) -> dict:
    seeds = jax.random.split(jax.random.key(seed), 17)
    return {
        "encoded": normal_values(seeds[0], (SAMPLES, SEQ, D), 1.0, 6.0, ((0, 4), (1, 4))),
        "sent_forward": normal_values(seeds[1], (SECTIONS, SAMPLES, SEQ, D), 1.0, 6.0, ((0, 2), (1, 4), (2, 4))),
        "head_cotangent": normal_values(seeds[2], (SAMPLES, SEQ, D), 1.0, 6.0, ((0, 4), (1, 4))),
        "grad_sent": normal_values(seeds[3], (SECTIONS, SAMPLES, SEQ, D), 1.0, 6.0, ((0, 2), (1, 4), (2, 4))),
        "x_saved": normal_values(seeds[4], (SECTIONS, SAMPLES, SEQ, D), 1.0, 6.0, ((0, 2), (1, 4), (2, 4))),
        "q_saved": normal_values(seeds[5], (SECTIONS, SAMPLES, SEQ, HEADS * HD), 1.0, 6.0, ((0, 2), (1, 4), (3, 4))),
        "k_saved": normal_values(seeds[6], (SECTIONS, SAMPLES, SEQ, HEADS * HD), 1.0, 6.0, ((0, 2), (1, 4), (3, 4))),
        "v_saved": normal_values(seeds[7], (SECTIONS, SAMPLES, SEQ, HEADS * HD), 1.0, 6.0, ((0, 2), (1, 4), (3, 4))),
        "norm_gain": jnp.clip(1.0 + 0.15 * jax.random.normal(seeds[8], (SECTIONS, D), jnp.float32), 0.25, 1.75),
        "logit_scale": draw_logit_scale(jax.random.fold_in(seeds[16], 71), 0),
        "w_query": normal_values(seeds[10], (SECTIONS, D, HEADS * HD), D ** -0.5, 0.09375, ((0, 2), (2, 4))),
        "w_key": normal_values(seeds[11], (SECTIONS, D, HEADS * HD), D ** -0.5, 0.09375, ((0, 2), (2, 4))),
        "w_value": normal_values(seeds[12], (SECTIONS, D, HEADS * HD), D ** -0.5, 0.09375, ((0, 2), (2, 4))),
        "w_out": normal_values(seeds[13], (SECTIONS, HEADS * HD, D), HD ** -0.5, 0.5, ((0, 2), (1, 4))),
        "key_blocks": draw_key_blocks(jax.random.fold_in(seeds[16], 71), 0),
        "key_counts": draw_key_counts(jax.random.fold_in(seeds[16], 71), 0),
    }


epsilon = 1e-05

def normalize(rows_in, gain_row):
    widened = rows_in.astype(jnp.float32)
    inverse_rms = lax.rsqrt(lax.optimization_barrier(jnp.mean(widened * widened, axis=-1, keepdims=True)) + epsilon)
    unit_rows = widened * inverse_rms
    return ((unit_rows * gain_row).astype(jnp.bfloat16), inverse_rms, unit_rows)

def gather_sets(tensor, block_ids):
    block_count, slot_count = block_ids.shape
    blocks = tensor.reshape(block_count, BLOCK, tensor.shape[1], tensor.shape[2])
    return blocks[block_ids].reshape(block_count, slot_count * BLOCK, tensor.shape[1], tensor.shape[2])

def attention_parts(queries, key_rows, value_rows, factor, block_ids, counts):
    block_count, slot_count = block_ids.shape
    query_blocks = queries.reshape(block_count, BLOCK, queries.shape[1], queries.shape[2]).astype(jnp.float32)
    key_sets = gather_sets(key_rows, block_ids).astype(jnp.float32)
    value_sets = gather_sets(value_rows, block_ids).astype(jnp.float32)
    live_slots = jnp.arange(slot_count, dtype=jnp.int32)[None, :] < counts[:, None]
    allowed = jnp.repeat(live_slots, BLOCK, axis=1)
    scores = jnp.einsum('qihd,qjhd->qhij', query_blocks, key_sets) * factor[None, :, None, None]
    scores = jnp.where(allowed[:, None, None, :], scores, -1e+30)
    row_max = lax.optimization_barrier(jnp.max(scores, axis=-1, keepdims=True))
    lifted = jnp.exp(scores - row_max)
    soft = lifted / lax.optimization_barrier(jnp.sum(lifted, axis=-1, keepdims=True))
    rounded = soft.astype(jnp.bfloat16)
    attended = jnp.einsum('qhij,qjhd->qihd', rounded.astype(jnp.float32), value_sets).astype(jnp.bfloat16)
    return (soft, rounded, attended, query_blocks, key_sets, value_sets)

def attention_grads(queries, key_rows, value_rows, grad_attended, factor, block_ids, counts):
    soft, rounded, attended, query_blocks, key_sets, value_sets = attention_parts(queries, key_rows, value_rows, factor, block_ids, counts)
    block_count, slot_count = block_ids.shape
    head_count, head_width = (queries.shape[1], queries.shape[2])
    seq_len = block_count * BLOCK
    cot_blocks = grad_attended.reshape(block_count, BLOCK, head_count, head_width).astype(jnp.float32)
    grad_probs = jnp.einsum('qihd,qjhd->qhij', cot_blocks, value_sets)
    row_dots = lax.optimization_barrier(jnp.sum(cot_blocks * attended.astype(jnp.float32), axis=-1))
    row_dots = jnp.transpose(row_dots, (0, 2, 1))[..., None]
    grad_scores = (soft * (grad_probs - row_dots) * factor[None, :, None, None]).astype(jnp.bfloat16)
    query_grads = jnp.einsum('qhij,qjhd->qihd', grad_scores.astype(jnp.float32), key_sets).astype(jnp.bfloat16)
    key_terms = jnp.einsum('qhij,qihd->qjhd', grad_scores.astype(jnp.float32), query_blocks)
    value_terms = jnp.einsum('qhij,qihd->qjhd', rounded.astype(jnp.float32), cot_blocks)
    choose = (block_ids[:, :, None] == jnp.arange(block_count, dtype=jnp.int32)[None, None, :]).astype(jnp.float32)
    split_shape = (block_count, slot_count, BLOCK, head_count, head_width)
    key_grads = jnp.einsum('qkn,qkjhd->njhd', choose, key_terms.reshape(split_shape)).astype(jnp.bfloat16)
    value_grads = jnp.einsum('qkn,qkjhd->njhd', choose, value_terms.reshape(split_shape)).astype(jnp.bfloat16)
    flat_width = head_count * head_width
    return (attended.reshape(seq_len, flat_width), query_grads.reshape(seq_len, flat_width), key_grads.reshape(seq_len, flat_width), value_grads.reshape(seq_len, flat_width))

def rounded_sum(terms):
    return lax.optimization_barrier(terms.astype(jnp.bfloat16)).astype(jnp.float32).sum(axis=0)

def reference(encoded, sent_forward, head_cotangent, grad_sent, x_saved, q_saved, k_saved, v_saved, norm_gain, logit_scale, w_query, w_key, w_value, w_out, key_blocks, key_counts):
    group_width = HEADS * HD // N_SEQ
    forward_rows, back_rows = ([], [])
    grads_query, grads_key, grads_value, grads_out, grads_gain = ([], [], [], [], [])
    for section_id in range(SECTIONS):
        gain_row = norm_gain[section_id].astype(jnp.float32)
        factor = logit_scale[section_id].astype(jnp.float32) / math.sqrt(HD)
        query_weight, key_weight, value_weight, out_weight = (w_query[section_id], w_key[section_id], w_value[section_id], w_out[section_id])
        out_groups = out_weight.reshape(N_SEQ, group_width, D).astype(jnp.float32)
        query_groups = query_weight.reshape(D, N_SEQ, group_width).astype(jnp.float32)
        key_groups = key_weight.reshape(D, N_SEQ, group_width).astype(jnp.float32)
        value_groups = value_weight.reshape(D, N_SEQ, group_width).astype(jnp.float32)
        totals = [jnp.zeros((D, HEADS * HD), jnp.float32) for _ in range(3)]
        out_total = jnp.zeros((HEADS * HD, D), jnp.float32)
        gain_total = jnp.zeros((D,), jnp.float32)
        section_forward, section_back = ([], [])
        for sample in range(SAMPLES):
            block_ids = key_blocks[sample]
            counts = key_counts[sample]
            section_in = encoded[sample] if section_id == 0 else sent_forward[section_id - 1, sample]
            cot_in = head_cotangent[sample] if section_id == SECTIONS - 1 else grad_sent[section_id + 1, sample]
            normed, _, _ = normalize(section_in, gain_row)
            queries = jnp.dot(normed, query_weight, preferred_element_type=jnp.float32).astype(jnp.bfloat16)
            key_rows = jnp.dot(normed, key_weight, preferred_element_type=jnp.float32).astype(jnp.bfloat16)
            value_rows = jnp.dot(normed, value_weight, preferred_element_type=jnp.float32).astype(jnp.bfloat16)
            shaped = (SEQ, HEADS, HD)
            attended = attention_parts(queries.reshape(shaped), key_rows.reshape(shaped), value_rows.reshape(shaped), factor, block_ids, counts)[2]
            attended = attended.reshape(SEQ, N_SEQ, group_width).astype(jnp.float32)
            mixed = rounded_sum(jnp.einsum('tgc,gcd->gtd', attended, out_groups))
            section_forward.append((section_in.astype(jnp.float32) + mixed).astype(jnp.bfloat16))
            saved_normed, inverse_rms, unit_rows = normalize(x_saved[section_id, sample], gain_row)
            grad_attended = jnp.dot(cot_in, out_weight.T, preferred_element_type=jnp.float32).astype(jnp.bfloat16)
            saved_attended, query_grads, key_grads, value_grads = attention_grads(q_saved[section_id, sample].reshape(shaped), k_saved[section_id, sample].reshape(shaped), v_saved[section_id, sample].reshape(shaped), grad_attended.reshape(shaped), factor, block_ids, counts)
            for index, grads in enumerate((query_grads, key_grads, value_grads)):
                term = jnp.dot(saved_normed.T, grads, preferred_element_type=jnp.float32)
                totals[index] = totals[index] + lax.optimization_barrier(term.astype(jnp.bfloat16)).astype(jnp.float32)
            term = jnp.dot(saved_attended.T, cot_in, preferred_element_type=jnp.float32)
            out_total = out_total + lax.optimization_barrier(term.astype(jnp.bfloat16)).astype(jnp.float32)
            split = (SEQ, N_SEQ, group_width)
            input_terms = jnp.einsum('tgc,dgc->gtd', query_grads.reshape(split).astype(jnp.float32), query_groups)
            input_terms = input_terms + jnp.einsum('tgc,dgc->gtd', key_grads.reshape(split).astype(jnp.float32), key_groups)
            input_terms = input_terms + jnp.einsum('tgc,dgc->gtd', value_grads.reshape(split).astype(jnp.float32), value_groups)
            grad_normed = rounded_sum(input_terms)
            scaled = gain_row * grad_normed
            back = cot_in.astype(jnp.float32) + inverse_rms * (scaled - unit_rows * lax.optimization_barrier(jnp.mean(scaled * unit_rows, axis=-1, keepdims=True)))
            section_back.append(back.astype(jnp.bfloat16))
            gain_total = gain_total + lax.optimization_barrier(jnp.sum(grad_normed * unit_rows, axis=0))
        forward_rows.append(jnp.stack(section_forward))
        back_rows.append(jnp.stack(section_back))
        grads_query.append(totals[0].astype(jnp.bfloat16))
        grads_key.append(totals[1].astype(jnp.bfloat16))
        grads_value.append(totals[2].astype(jnp.bfloat16))
        grads_out.append(out_total.astype(jnp.bfloat16))
        grads_gain.append(gain_total)
    return (jnp.stack(forward_rows), jnp.stack(back_rows), jnp.stack(grads_query), jnp.stack(grads_key), jnp.stack(grads_value), jnp.stack(grads_out), jnp.stack(grads_gain))
```

```python
import functools
import math

import jax
import jax.numpy as jnp
from jax import lax
from jax.experimental import pallas as pl
from jax.experimental.pallas import tpu as pltpu
from jax.sharding import PartitionSpec as P

HD = 128
BLOCK = 128
EPSILON = 1e-05
CHUNK = 512
MIB = 1024 * 1024

BF16 = jnp.bfloat16
F32 = jnp.float32
HBM = pl.BlockSpec(memory_space=pl.ANY)
SMEM = pl.BlockSpec(memory_space=pltpu.SMEM)


def dot_nn(a, b):
    return lax.dot_general(a, b, (((1,), (0,)), ((), ())), preferred_element_type=F32)


def dot_nt(a, b):
    return lax.dot_general(a, b, (((1,), (1,)), ((), ())), preferred_element_type=F32)


def dot_tn(a, b):
    return lax.dot_general(a, b, (((0,), (0,)), ((), ())), preferred_element_type=F32)


def sds(shape, dtype):
    return jax.ShapeDtypeStruct(shape, dtype)


def params(mib, grid=0):
    semantics = ("arbitrary",) * grid if grid else None
    return pltpu.CompilerParams(vmem_limit_bytes=mib * MIB, dimension_semantics=semantics)


def cost(flops, moved):
    return pl.CostEstimate(flops=int(flops), bytes_accessed=int(moved), transcendentals=0)


def run_copies(copies):
    for copy in copies:
        copy.start()
    for copy in copies:
        copy.wait()


def normalized(rows, gain):
    widened = rows.astype(F32)
    inverse = lax.rsqrt(jnp.mean(widened * widened, axis=-1, keepdims=True) + EPSILON)
    unit = widened * inverse
    return unit, inverse, (unit * gain).astype(BF16)


def seen_pairs(blocks_ref, counts_ref, tokens):
    count, slots = blocks_ref.shape
    row_block = lax.broadcasted_iota(jnp.int32, (tokens, tokens), 0) // BLOCK
    col_block = lax.broadcasted_iota(jnp.int32, (tokens, tokens), 1) // BLOCK
    seen = jnp.zeros((tokens, tokens), jnp.int32)
    for i in range(count):
        for j in range(count):
            flag = jnp.int32(0)
            for t in range(slots):
                listed = (t < counts_ref[i]) & (blocks_ref[i, t] == j)
                flag = flag | listed.astype(jnp.int32)
            seen = jnp.where((row_block == i) & (col_block == j), flag, seen)
    return seen


def soft_scores(query, key, factor, seen):
    scores = dot_nt(query, key) * factor
    scores = jnp.where(seen > 0, scores, -1e30)
    lifted = jnp.exp(scores - jnp.max(scores, axis=-1, keepdims=True))
    return lifted / jnp.sum(lifted, axis=-1, keepdims=True)


def pick_kernel(forward_ref, encoded_ref, grad_ref, head_ref, out_f, out_c, sem):
    section = lax.axis_index("pipe")

    def both(first, second):
        run_copies(
            [
                pltpu.make_async_copy(first, out_f, sem.at[0]),
                pltpu.make_async_copy(second, out_c, sem.at[1]),
            ]
        )

    @pl.when(section == 0)
    def _():
        both(forward_ref, head_ref)

    @pl.when(section != 0)
    def _():
        both(encoded_ref, grad_ref)


def pick(sent_forward, encoded, grad_sent, head):
    shape = encoded.shape
    return pl.pallas_call(
        pick_kernel,
        out_shape=(sds(shape, BF16), sds(shape, BF16)),
        in_specs=[HBM] * 4,
        out_specs=(HBM, HBM),
        scratch_shapes=[pltpu.SemaphoreType.DMA((2,))],
        cost_estimate=cost(0, 4 * encoded.size * 2),
        name="pick",
    )(sent_forward, encoded, grad_sent, head)


def columns_kernel(x_ref, cot_ref, gain_ref, *rest):
    outs, held = rest[:-1], rest[-1]
    me = lax.axis_index("dp")
    n = len(outs)
    width = outs[0].shape[-1]
    held[...] = normalized(x_ref[...], gain_ref[...])[2]
    for k, out in enumerate(outs):
        start = pl.multiple_of(lax.rem(me + k, n) * width, width)
        out[0] = held[:, pl.ds(start, width)]
        out[1] = cot_ref[:, pl.ds(start, width)]


def column_parts(x, cot, gain, n):
    rows, width = x.shape
    part = (2, rows, width // n)
    return pl.pallas_call(
        columns_kernel,
        out_shape=tuple(sds(part, BF16) for _ in range(n)),
        scratch_shapes=[pltpu.VMEM((rows, width), BF16)],
        compiler_params=params(16),
        cost_estimate=cost(0, 4 * x.size * 2),
        name="columns",
    )(x, cot, gain)


def saved_kernel(blocks_ref, counts_ref, factor_ref, q_ref, k_ref, v_ref, soft_ref, att_ref):
    tokens, width = q_ref.shape
    seen = seen_pairs(blocks_ref, counts_ref, tokens)
    for h in range(width // HD):
        cols = slice(h * HD, (h + 1) * HD)
        soft = soft_scores(q_ref[:, cols], k_ref[:, cols], factor_ref[0, h], seen)
        soft_ref[h] = soft
        att_ref[:, cols] = dot_nn(soft.astype(BF16), v_ref[:, cols]).astype(BF16)


def saved_attention(blocks, counts, factor, q, k, v):
    tokens, width = q.shape
    heads = width // HD
    return pl.pallas_call(
        saved_kernel,
        out_shape=(sds((heads, tokens, tokens), F32), sds((tokens, width), BF16)),
        in_specs=[SMEM] * 3 + [pl.BlockSpec(memory_space=pltpu.VMEM)] * 3,
        compiler_params=params(24),
        cost_estimate=cost(4 * tokens * tokens * width, 4 * heads * tokens * tokens),
        name="saved_attention",
    )(blocks, counts, factor, q, k, v)


def block_copies(refs, held, rows, sems):
    me = lax.axis_index("seq")
    copies = []
    for j, ref in enumerate(refs):
        at = pl.multiple_of((me ^ j) * rows, rows)
        copies.append(pltpu.make_async_copy(ref, held.at[pl.ds(at, rows)], sems.at[j]))
    return copies


def backward_kernel(
    n, factor_ref, *rest
):
    cots, rest = rest[:n], rest[n:]
    w_ref, soft_ref, att_ref, q_ref, k_ref, v_ref, out_ref, held, total, sems = rest
    step = pl.program_id(0)
    rows = cots[0].shape[0]
    tokens, width = q_ref.shape

    @pl.when(step == 0)
    def _():
        run_copies(block_copies(cots, held, rows, sems))
        total[...] = jnp.zeros_like(total)

    at = pl.multiple_of(step * CHUNK, CHUNK)
    total[...] += dot_nt(held[:, pl.ds(at, CHUNK)], w_ref[...])

    @pl.when(step == pl.num_programs(0) - 1)
    def _():
        for h in range(width // HD):
            cols = slice(h * HD, (h + 1) * HD)
            cot = total[:, cols].astype(BF16)
            soft = soft_ref[h]
            products = cot.astype(F32) * att_ref[:, cols].astype(F32)
            dots = jnp.sum(products, axis=-1, keepdims=True)
            grads = soft * (dot_nt(cot, v_ref[:, cols]) - dots) * factor_ref[0, h]
            grads = grads.astype(BF16)
            low = soft.astype(BF16)
            out_ref[:, h * HD : (h + 1) * HD] = dot_nn(grads, k_ref[:, cols]).astype(BF16)
            key_at = width + h * HD
            out_ref[:, key_at : key_at + HD] = dot_tn(grads, q_ref[:, cols]).astype(BF16)
            value_at = 2 * width + h * HD
            out_ref[:, value_at : value_at + HD] = dot_tn(low, cot).astype(BF16)


def backward_attention(factor, cots, w_out, soft, att, q, k, v):
    tokens, width = q.shape
    model = w_out.shape[1]
    n = len(cots)
    whole = lambda a: pl.BlockSpec(a.shape, lambda i: (0,) * a.ndim)
    return pl.pallas_call(
        functools.partial(backward_kernel, n),
        grid=(model // CHUNK,),
        out_shape=sds((tokens, 3 * width), BF16),
        in_specs=[SMEM]
        + [HBM] * n
        + [pl.BlockSpec((width, CHUNK), lambda i: (0, i))]
        + [whole(a) for a in (soft, att, q, k, v)],
        out_specs=pl.BlockSpec((tokens, 3 * width), lambda i: (0, 0)),
        scratch_shapes=[
            pltpu.VMEM((tokens, model), BF16),
            pltpu.VMEM((tokens, width), F32),
            pltpu.SemaphoreType.DMA((n,)),
        ],
        compiler_params=params(28, 1),
        cost_estimate=cost(2 * tokens * model * width, 2 * w_out.size + 8 * MIB),
        name="backward_attention",
    )(factor, *cots, w_out, soft, att, q, k, v)


def input_grad_kernel(g_ref, wq_ref, wk_ref, wv_ref, *rest):
    outs, held = rest[:-1], rest[-1]
    width = wq_ref.shape[1]
    total = dot_nt(g_ref[:, :width], wq_ref[...])
    total += dot_nt(g_ref[:, width : 2 * width], wk_ref[...])
    total += dot_nt(g_ref[:, 2 * width :], wv_ref[...])
    held[...] = total.astype(BF16)
    rows = outs[0].shape[0]
    me = lax.axis_index("seq")
    for j, out in enumerate(outs):
        out[...] = held[pl.ds(pl.multiple_of((me ^ j) * rows, rows), rows), :]


def input_grads(grads, wq, wk, wv, n):
    tokens = grads.shape[0]
    model, width = wq.shape
    rows = tokens // n
    tile = pl.BlockSpec((CHUNK, width), lambda i: (i, 0))
    return pl.pallas_call(
        input_grad_kernel,
        grid=(model // CHUNK,),
        out_shape=tuple(sds((rows, model), BF16) for _ in range(n)),
        in_specs=[pl.BlockSpec(grads.shape, lambda i: (0, 0)), tile, tile, tile],
        out_specs=tuple(pl.BlockSpec((rows, CHUNK), lambda i: (0, i)) for _ in range(n)),
        scratch_shapes=[pltpu.VMEM((tokens, CHUNK), BF16)],
        compiler_params=params(20, 1),
        cost_estimate=cost(6 * tokens * model * width, 6 * wq.size),
        name="input_grads",
    )(grads, wq, wk, wv)


def forward_kernel(n, blocks_ref, counts_ref, factor_ref, *rest):
    xs, rest = rest[:n], rest[n:]
    gain_ref, wq_ref, wk_ref, wv_ref, wo_ref = rest[:5]
    outs, rest = rest[5 : 5 + n], rest[5 + n :]
    held, wo, tq, tk, tv, att, sems = rest
    step = pl.program_id(0)
    rows = xs[0].shape[0]
    me = lax.axis_index("seq")
    load_wo = pltpu.make_async_copy(wo_ref, wo, sems.at[n])

    @pl.when(step == 0)
    def _():
        copies = block_copies(xs, held, rows, sems)
        for copy in copies:
            copy.start()
        load_wo.start()
        for copy in copies:
            copy.wait()

        @pl.loop(0, held.shape[0] // 32)
        def _(i):
            at = pl.ds(pl.multiple_of(i * 32, 32), 32)
            held[at, :] = normalized(held[at, :], gain_ref[...])[2]

        for total in (tq, tk, tv):
            total[...] = jnp.zeros_like(total)

    part = held[:, pl.ds(pl.multiple_of(step * CHUNK, CHUNK), CHUNK)]
    tq[...] += dot_nn(part, wq_ref[...])
    tk[...] += dot_nn(part, wk_ref[...])
    tv[...] += dot_nn(part, wv_ref[...])

    @pl.when(step == pl.num_programs(0) - 1)
    def _():
        tokens, width = tq.shape
        seen = seen_pairs(blocks_ref, counts_ref, tokens)
        for h in range(width // HD):
            cols = slice(h * HD, (h + 1) * HD)
            query, key, value = (t[:, cols].astype(BF16) for t in (tq, tk, tv))
            soft = soft_scores(query, key, factor_ref[0, h], seen)
            att[:, cols] = dot_nn(soft.astype(BF16), value).astype(BF16)
        load_wo.wait()

        @pl.loop(0, wo.shape[1] // CHUNK)
        def _(i):
            at = pl.ds(pl.multiple_of(i * CHUNK, CHUNK), CHUNK)
            held[:, at] = dot_nn(att[...], wo[:, at]).astype(BF16)

        for j, out in enumerate(outs):
            out[...] = held[pl.ds(pl.multiple_of((me ^ j) * rows, rows), rows), :]


def forward_terms(blocks, counts, factor, xs, gain, wq, wk, wv, wo):
    n = len(xs)
    rows, model = xs[0].shape
    width = wq.shape[1]
    tokens = rows * n
    tile = pl.BlockSpec((CHUNK, width), lambda i: (i, 0))
    return pl.pallas_call(
        functools.partial(forward_kernel, n),
        grid=(model // CHUNK,),
        out_shape=tuple(sds((rows, model), BF16) for _ in range(n)),
        in_specs=[SMEM] * 3
        + [HBM] * n
        + [pl.BlockSpec((1, model), lambda i: (0, 0)), tile, tile, tile, HBM],
        out_specs=tuple(pl.BlockSpec((rows, model), lambda i: (0, 0)) for _ in range(n)),
        scratch_shapes=[
            pltpu.VMEM((tokens, model), BF16),
            pltpu.VMEM((width, model), BF16),
        ]
        + [pltpu.VMEM((tokens, width), F32)] * 3
        + [pltpu.VMEM((tokens, width), BF16), pltpu.SemaphoreType.DMA((n + 1,))],
        compiler_params=params(36, 1),
        cost_estimate=cost(8 * tokens * model * width, 8 * wq.size),
        name="forward_terms",
    )(blocks, counts, factor, *xs, gain, wq, wk, wv, wo)


def back_kernel(n, *rest):
    terms, rest = rest[:n], rest[n:]
    x_ref, cot_ref, gain_ref, back_ref, part_ref = rest
    gain = gain_ref[...]
    unit, inverse, _ = normalized(x_ref[...], gain)
    grad = terms[0][...].astype(F32)
    for term in terms[1:]:
        grad += term[...].astype(F32)
    scaled = gain * grad
    part_ref[...] = jnp.sum(grad * unit, axis=0, keepdims=True)
    inner = jnp.mean(scaled * unit, axis=-1, keepdims=True)
    back_ref[...] = (cot_ref[...].astype(F32) + inverse * (scaled - unit * inner)).astype(BF16)


def back(terms, x, cot, gain):
    return pl.pallas_call(
        functools.partial(back_kernel, len(terms)),
        out_shape=(sds(x.shape, BF16), sds(gain.shape, F32)),
        compiler_params=params(24),
        cost_estimate=cost(0, 7 * x.size * 2),
        name="back",
    )(*terms, x, cot, gain)


def column_copies(parts, which, held, sems):
    me = lax.axis_index("seq")
    copies = []
    for j, part in enumerate(parts):
        rows = part.shape[2]
        at = pl.multiple_of((me ^ j) * rows, rows)
        copies.append(
            pltpu.make_async_copy(part.at[:, which], held.at[:, pl.ds(at, rows)], sems.at[j])
        )
    return copies


def weight_kernel(n_seq, n_dp, *rest):
    parts, rest = rest[:n_seq], rest[n_seq:]
    own, rest = rest[0], rest[1:]
    lower, rest = rest[: n_dp - 1], rest[n_dp - 1 :]
    upper, rest = rest[: n_dp - 1], rest[n_dp - 1 :]
    out_q, out_k, out_v, cols, grads, sems, own_sems = rest
    me = lax.axis_index("dp")

    def grad_copies(k, act):
        if k == 0:
            act(pltpu.make_async_copy(own, grads.at[0], own_sems.at[0]))
            return

        @pl.when(me >= k)
        def _():
            act(pltpu.make_async_copy(lower[k - 1], grads.at[k], own_sems.at[k]))

        @pl.when(me < k)
        def _():
            act(pltpu.make_async_copy(upper[n_dp - k - 1], grads.at[k], own_sems.at[k]))

    for k in range(n_dp):
        grad_copies(k, lambda copy: copy.start())
    run_copies(column_copies(parts, 0, cols, sems))
    for k in range(n_dp):
        grad_copies(k, lambda copy: copy.wait())
    width = out_q.shape[1]
    tile = min(256, out_q.shape[0])
    tokens = cols.shape[1]

    @pl.loop(0, out_q.shape[0] // tile)
    def _(i):
        at = pl.ds(pl.multiple_of(i * tile, tile), tile)
        total = dot_tn(
            cols[:, :, at].reshape(n_dp * tokens, tile),
            grads[...].reshape(n_dp * tokens, 3 * width),
        ).astype(BF16)
        out_q[at, :] = total[:, :width]
        out_k[at, :] = total[:, width : 2 * width]
        out_v[at, :] = total[:, 2 * width :]


def weight_grads(parts, own, lower, upper):
    n_dp, _, rows, slice_width = parts[0].shape
    tokens, triple = own.shape
    width = triple // 3
    held_mib = n_dp * tokens * (slice_width + triple) * 2 // MIB
    return pl.pallas_call(
        functools.partial(weight_kernel, len(parts), n_dp),
        out_shape=tuple(sds((slice_width, width), BF16) for _ in range(3)),
        in_specs=[HBM] * (len(parts) + 2 * n_dp - 1),
        scratch_shapes=[
            pltpu.VMEM((n_dp, tokens, slice_width), BF16),
            pltpu.VMEM((n_dp, tokens, triple), BF16),
            pltpu.SemaphoreType.DMA((len(parts),)),
            pltpu.SemaphoreType.DMA((n_dp,)),
        ],
        compiler_params=params(min(60, held_mib + 24)),
        cost_estimate=cost(2 * n_dp * tokens * slice_width * triple, 8 * MIB),
        name="weight_grads",
    )(*parts, own, *lower, *upper)


def out_weight_kernel(n_seq, n_dp, *rest):
    parts, rest = rest[:n_seq], rest[n_seq:]
    atts, rest = rest[:n_dp], rest[n_dp:]
    out_ref, cols, held, sems, own_sems = rest
    copies = column_copies(parts, 1, cols, sems)
    for k, att in enumerate(atts):
        copies.append(pltpu.make_async_copy(att, held.at[k], own_sems.at[k]))
    run_copies(copies)
    tokens = cols.shape[1]
    tile = 128

    @pl.loop(0, out_ref.shape[0] // tile)
    def _(i):
        at = pl.ds(pl.multiple_of(i * tile, tile), tile)
        out_ref[at, :] = dot_tn(
            held[:, :, at].reshape(n_dp * tokens, tile),
            cols[...].reshape(n_dp * tokens, out_ref.shape[1]),
        ).astype(BF16)


def out_weight_grads(parts, atts):
    n_dp, _, rows, slice_width = parts[0].shape
    tokens, width = atts[0].shape
    held_mib = n_dp * tokens * (slice_width + width) * 2 // MIB
    return pl.pallas_call(
        functools.partial(out_weight_kernel, len(parts), n_dp),
        out_shape=sds((width, slice_width), BF16),
        in_specs=[HBM] * (len(parts) + n_dp),
        scratch_shapes=[
            pltpu.VMEM((n_dp, tokens, slice_width), BF16),
            pltpu.VMEM((n_dp, tokens, width), BF16),
            pltpu.SemaphoreType.DMA((len(parts),)),
            pltpu.SemaphoreType.DMA((n_dp,)),
        ],
        compiler_params=params(min(60, held_mib + 20)),
        cost_estimate=cost(2 * n_dp * tokens * slice_width * width, 5 * MIB),
        name="out_weight_grads",
    )(*parts, *atts)


def swapped(value, axis, j):
    return lax.ppermute(value, axis, [(i, i ^ j) for i in range(lax.axis_size(axis))])


def crossed(value, j):
    n = lax.axis_size("seq")
    pairs = [(p * n + i, (1 - p) * n + (i ^ j)) for p in range(2) for i in range(n)]
    return lax.ppermute(value, ("pipe", "seq"), pairs)


def rotated(value, axis, k):
    n = lax.axis_size(axis)
    return lax.ppermute(value, axis, [(i, (i + k) % n) for i in range(n)])


def shifted(value, axis, by):
    n = lax.axis_size(axis)
    return lax.ppermute(value, axis, [(i, i + by) for i in range(n) if 0 <= i + by < n])


def line_gather(value, axis):
    lower, upper, up, down = [], [], value, value
    for _ in range(lax.axis_size(axis) - 1):
        up, down = shifted(up, axis, 1), shifted(down, axis, -1)
        lower.append(up)
        upper.append(down)
    return lower, upper


def local(
    encoded,
    sent_forward,
    head_cotangent,
    grad_sent,
    x_saved,
    q_saved,
    k_saved,
    v_saved,
    norm_gain,
    logit_scale,
    w_query,
    w_key,
    w_value,
    w_out,
    key_blocks,
    key_counts,
):
    n_seq, n_dp = lax.axis_size("seq"), lax.axis_size("dp")
    factor = logit_scale / math.sqrt(HD)
    blocks, counts = key_blocks[0], key_counts[0]
    wq, wk, wv, wo = w_query[0], w_key[0], w_value[0], w_out[0]
    q, k, v, x = q_saved[0, 0], k_saved[0, 0], v_saved[0, 0], x_saved[0, 0]

    send_x, send_cot = pick(sent_forward[0, 0], encoded[0], grad_sent[0, 0], head_cotangent[0])
    cots = [crossed(send_cot, j) for j in range(n_seq)]
    xs = [crossed(send_x, j) for j in range(n_seq)]

    soft, att = saved_attention(blocks, counts, factor, q, k, v)
    columns = column_parts(x, cots[0], norm_gain, n_dp)
    columns = [columns[0]] + [rotated(columns[i], "dp", i) for i in range(1, n_dp)]
    atts = [att] + [rotated(att, "dp", i) for i in range(1, n_dp)]

    grads = backward_attention(factor, cots, wo, soft, att, q, k, v)
    lower, upper = line_gather(grads, "dp")
    dx = input_grads(grads, wq, wk, wv, n_seq)
    dx = [dx[0]] + [swapped(dx[j], "seq", j) for j in range(1, n_seq)]

    mixed = forward_terms(blocks, counts, factor, xs, norm_gain, wq, wk, wv, wo)
    mixed = [mixed[0]] + [swapped(mixed[j], "seq", j) for j in range(1, n_seq)]

    parts = jnp.stack(columns)
    parts = [parts] + [swapped(parts, "seq", j) for j in range(1, n_seq)]

    back_out, gain_part = back(dx, x, cots[0], norm_gain)
    for axis in ("seq", "dp"):
        hop = 1
        while hop < lax.axis_size(axis):
            gain_part = gain_part + swapped(gain_part, axis, hop)
            hop *= 2

    total = mixed[0].astype(F32)
    for term in mixed[1:]:
        total = total + term.astype(F32)
    forward_out = (xs[0].astype(F32) + total).astype(BF16)

    grad_out = out_weight_grads(parts, atts)
    grad_q, grad_k, grad_v = weight_grads(parts, grads, lower, upper)
    return (
        forward_out[None, None],
        back_out[None, None],
        grad_q[None],
        grad_k[None],
        grad_v[None],
        grad_out[None],
        gain_part,
    )


def solution(mesh):
    in_specs = (
        P("dp", "seq", None),
        P("pipe", "dp", "seq", None),
        P("dp", "seq", None),
        P("pipe", "dp", "seq", None),
        P("pipe", "dp", "seq", None),
        P("pipe", "dp", None, "seq"),
        P("pipe", "dp", None, "seq"),
        P("pipe", "dp", None, "seq"),
        P("pipe", None),
        P("pipe", "seq"),
        P("pipe", None, "seq"),
        P("pipe", None, "seq"),
        P("pipe", None, "seq"),
        P("pipe", "seq", None),
        P("dp", None, None),
        P("dp", None),
    )
    out_specs = (
        P("pipe", "dp", "seq", None),
        P("pipe", "dp", "seq", None),
        P("pipe", "dp", "seq"),
        P("pipe", "dp", "seq"),
        P("pipe", "dp", "seq"),
        P("pipe", "seq", "dp"),
        P("pipe", None),
    )
    return jax.shard_map(local, mesh=mesh, in_specs=in_specs, out_specs=out_specs, check_vma=False)
```

```python
import functools
import math

import jax
import jax.numpy as jnp
from jax import lax
from jax.experimental import pallas as pl
from jax.experimental.pallas import tpu as pltpu
from jax.sharding import PartitionSpec as P

HD = 128
BLOCK = 128
EPSILON = 1e-05
CHUNK = 512
MIB = 1024 * 1024

BF16 = jnp.bfloat16
F32 = jnp.float32
HBM = pl.BlockSpec(memory_space=pl.ANY)
VMEM = pl.BlockSpec(memory_space=pltpu.VMEM)
SMEM = pl.BlockSpec(memory_space=pltpu.SMEM)


def dot_nn(a, b):
    return lax.dot_general(a, b, (((1,), (0,)), ((), ())), preferred_element_type=F32)


def dot_nt(a, b):
    return lax.dot_general(a, b, (((1,), (1,)), ((), ())), preferred_element_type=F32)


def dot_tn(a, b):
    return lax.dot_general(a, b, (((0,), (0,)), ((), ())), preferred_element_type=F32)


def sds(shape, dtype):
    return jax.ShapeDtypeStruct(shape, dtype)


def params(grid=0):
    semantics = ("arbitrary",) * grid if grid else None
    return pltpu.CompilerParams(vmem_limit_bytes=64 * MIB, dimension_semantics=semantics)


SMALL = pl.CostEstimate(flops=1024, bytes_accessed=1024, transcendentals=0)


def run_copies(copies):
    for copy in copies:
        copy.start()
    for copy in copies:
        copy.wait()


def normalized(rows, gain):
    widened = rows.astype(F32)
    inverse = lax.rsqrt(jnp.mean(widened * widened, axis=-1, keepdims=True) + EPSILON)
    unit = widened * inverse
    return unit, inverse, (unit * gain).astype(BF16)


def seen_pairs(blocks_ref, counts_ref, tokens):
    count, slots = blocks_ref.shape
    row_block = lax.broadcasted_iota(jnp.int32, (tokens, tokens), 0) // BLOCK
    col_block = lax.broadcasted_iota(jnp.int32, (tokens, tokens), 1) // BLOCK
    seen = jnp.zeros((tokens, tokens), jnp.int32)
    for i in range(count):
        for j in range(count):
            flag = jnp.int32(0)
            for t in range(slots):
                listed = (t < counts_ref[i]) & (blocks_ref[i, t] == j)
                flag = flag | listed.astype(jnp.int32)
            seen = jnp.where((row_block == i) & (col_block == j), flag, seen)
    return seen


def soft_scores(query, key, factor, seen):
    scores = dot_nt(query, key) * factor
    scores = jnp.where(seen > 0, scores, -1e30)
    lifted = jnp.exp(scores - jnp.max(scores, axis=-1, keepdims=True))
    return lifted / jnp.sum(lifted, axis=-1, keepdims=True)


def pick_kernel(forward_ref, encoded_ref, grad_ref, head_ref, out_ref, sems):
    section = lax.axis_index("pipe")

    def both(first, second):
        run_copies(
            [
                pltpu.make_async_copy(first, out_ref.at[0], sems.at[0]),
                pltpu.make_async_copy(second, out_ref.at[1], sems.at[1]),
            ]
        )

    @pl.when(section == 0)
    def _():
        both(head_ref, forward_ref)

    @pl.when(section != 0)
    def _():
        both(grad_ref, encoded_ref)


def pick(sent_forward, encoded, grad_sent, head):
    return pl.pallas_call(
        pick_kernel,
        out_shape=sds((2,) + encoded.shape, BF16),
        in_specs=[HBM] * 4,
        scratch_shapes=[pltpu.SemaphoreType.DMA((2,))],
        compiler_params=params(),
        cost_estimate=SMALL,
        name="pick",
    )(sent_forward, encoded, grad_sent, head)


def columns_kernel(x_ref, ins_ref, gain_ref, *rest):
    outs, held = rest[:-1], rest[-1]
    me = lax.axis_index("dp")
    n = len(outs)
    width = outs[0].shape[-1]
    held[...] = normalized(x_ref[...], gain_ref[...])[2]
    for k, out in enumerate(outs):
        start = pl.multiple_of(lax.rem(me + k, n) * width, width)
        out[0] = held[:, pl.ds(start, width)]
        out[1] = ins_ref[0, :, pl.ds(start, width)]


def column_parts(x, ins, gain, n):
    rows, width = x.shape
    part = (2, rows, width // n)
    return pl.pallas_call(
        columns_kernel,
        out_shape=tuple(sds(part, BF16) for _ in range(n)),
        scratch_shapes=[pltpu.VMEM((rows, width), BF16)],
        compiler_params=params(),
        cost_estimate=SMALL,
        name="columns",
    )(x, ins, gain)


def saved_kernel(blocks_ref, counts_ref, factor_ref, q_ref, k_ref, v_ref, *rest):
    soft_ref, att_ref = rest[-2:]
    tokens, width = q_ref.shape
    seen = seen_pairs(blocks_ref, counts_ref, tokens)
    for h in range(width // HD):
        cols = slice(h * HD, (h + 1) * HD)
        soft = soft_scores(q_ref[:, cols], k_ref[:, cols], factor_ref[0, h], seen)
        soft_ref[h] = soft
        att_ref[:, cols] = dot_nn(soft.astype(BF16), v_ref[:, cols]).astype(BF16)


def saved_attention(blocks, counts, factor, q, k, v, after=()):
    tokens, width = q.shape
    heads = width // HD
    return pl.pallas_call(
        saved_kernel,
        out_shape=(sds((heads, tokens, tokens), F32), sds((tokens, width), BF16)),
        in_specs=[SMEM] * 3 + [VMEM] * 3 + [HBM] * len(after),
        compiler_params=params(),
        cost_estimate=SMALL,
        name="saved_attention",
    )(blocks, counts, factor, q, k, v, *after)


def placed(refs, which):
    return [ref.at[which] for ref in refs[:3]] + [refs[3]]


def block_copies(refs, which, held, sems):
    me = lax.axis_index("seq")
    rows = refs[0].shape[1]
    copies = []
    for j, ref in enumerate(refs):
        at = (me ^ min(j, 3)) * rows + (rows // 2 if j == 4 else 0)
        spot = held.at[pl.ds(pl.multiple_of(at, rows // 2), ref.shape[1])]
        copies.append(pltpu.make_async_copy(ref.at[which], spot, sems.at[j]))
    return copies


def split_rows(held, near_ref, far_ref, first, second, cols_in, cols_out):
    me = lax.axis_index("seq")
    rows = near_ref.shape[1]
    for ref, hop in ((near_ref, 0), (far_ref, first)):
        for i, other in enumerate((0, second)):
            at = pl.multiple_of((me ^ hop ^ other) * rows, rows)
            ref[i, :, cols_out] = held[pl.ds(at, rows), cols_in]


def chunk_loads(source, held, sems, rows):
    return [
        pltpu.make_async_copy(
            source.at[pl.ds(i * rows, rows)], held.at[pl.ds(i * rows, rows)], sems.at[i]
        )
        for i in range(source.shape[0] // rows)
    ]


def backward_kernel(n, factor_ref, *rest):
    cots, rest = rest[:n], rest[n:]
    w_ref, soft_in, att_ref, q_ref, k_ref, v_ref, rest = *rest[:6], rest[6:]
    out_ref, held, w, soft_ref, sems, w_sems = rest[-6:]
    rows = cots[0].shape[1]
    tokens, width = q_ref.shape
    copies = block_copies(cots, 0, held, sems)
    for copy in copies:
        copy.start()
    loads = chunk_loads(w_ref, w, w_sems, HD)
    for load in loads:
        load.start()
    load_soft = pltpu.make_async_copy(soft_in, soft_ref, w_sems.at[len(loads)])
    load_soft.start()
    for copy in copies:
        copy.wait()
    for h in range(width // HD):
        loads[h].wait()
        cols = slice(h * HD, (h + 1) * HD)
        cot = dot_nt(held[...], w[cols, :]).astype(BF16)
        if h == 0:
            load_soft.wait()
        soft = soft_ref[h]
        products = cot.astype(F32) * att_ref[:, cols].astype(F32)
        dots = jnp.sum(products, axis=-1, keepdims=True)
        grads = soft * (dot_nt(cot, v_ref[:, cols]) - dots) * factor_ref[0, h]
        grads = grads.astype(BF16)
        low = soft.astype(BF16)
        out_ref[:, h * HD : (h + 1) * HD] = dot_nn(grads, k_ref[:, cols]).astype(BF16)
        key_at = width + h * HD
        out_ref[:, key_at : key_at + HD] = dot_tn(grads, q_ref[:, cols]).astype(BF16)
        value_at = 2 * width + h * HD
        out_ref[:, value_at : value_at + HD] = dot_tn(low, cot).astype(BF16)


def backward_attention(factor, cots, w_out, soft, att, q, k, v, after=()):
    tokens, width = q.shape
    model = w_out.shape[1]
    n = len(cots)
    return pl.pallas_call(
        functools.partial(backward_kernel, n),
        out_shape=sds((tokens, 3 * width), BF16),
        in_specs=[SMEM] + [HBM] * (n + 2) + [VMEM] * 4 + [HBM] * len(after),
        scratch_shapes=[
            pltpu.VMEM((tokens, model), BF16),
            pltpu.VMEM(w_out.shape, BF16),
            pltpu.VMEM(soft.shape, F32),
            pltpu.SemaphoreType.DMA((n,)),
            pltpu.SemaphoreType.DMA((width // HD + 1,)),
        ],
        compiler_params=params(),
        cost_estimate=SMALL,
        name="backward_attention",
    )(factor, *cots, w_out, soft, att, q, k, v, *after)


def input_grad_kernel(n_after, g_ref, *rest):
    weights, rest = rest[:3], rest[3 + n_after :]
    near_ref, far_ref, held, wq, wk, wv, sems = rest
    width = wq.shape[1]
    loads = [
        chunk_loads(source, w, sems.at[i], CHUNK)
        for i, (source, w) in enumerate(zip(weights, (wq, wk, wv)))
    ]
    for group in zip(*loads):
        for load in group:
            load.start()
    for i, group in enumerate(zip(*loads)):
        for load in group:
            load.wait()
        at = slice(i * CHUNK, (i + 1) * CHUNK)
        total = dot_nt(g_ref[:, :width], wq[at, :])
        total += dot_nt(g_ref[:, width : 2 * width], wk[at, :])
        total += dot_nt(g_ref[:, 2 * width :], wv[at, :])
        held[...] = total.astype(BF16)
        split_rows(held, near_ref, far_ref, 1, 2, slice(None), at)


def input_grads(grads, wq, wk, wv, after=()):
    tokens = grads.shape[0]
    model, width = wq.shape
    rows = tokens // 4
    return pl.pallas_call(
        functools.partial(input_grad_kernel, len(after)),
        out_shape=(sds((2, rows, model), BF16),) * 2,
        in_specs=[VMEM] + [HBM] * (3 + len(after)),
        scratch_shapes=[pltpu.VMEM((tokens, CHUNK), BF16)]
        + [pltpu.VMEM(wq.shape, BF16)] * 3
        + [pltpu.SemaphoreType.DMA((3, model // CHUNK))],
        compiler_params=params(),
        cost_estimate=SMALL,
        name="input_grads",
    )(grads, wq, wk, wv, *after)


def forward_kernel(n, n_after, blocks_ref, counts_ref, factor_ref, *rest):
    xs, rest = rest[:n], rest[n:]
    gain_ref, weights, wo_ref = rest[0], rest[1:4], rest[4]
    rest = rest[5 + n_after :]
    near_ref, far_ref, held, wq, wk, wv, wo, tq, tk, tv, att, x_sems, sems = rest
    rows = xs[0].shape[1]
    copies = block_copies(xs, 1, held, x_sems)
    loads = [
        chunk_loads(source, w, sems.at[i], CHUNK)
        for i, (source, w) in enumerate(zip(weights, (wq, wk, wv)))
    ]
    load_wo = pltpu.make_async_copy(wo_ref, wo, x_sems.at[n])
    for copy in copies:
        copy.start()
    for group in zip(*loads):
        for load in group:
            load.start()
    load_wo.start()
    for copy in copies:
        copy.wait()

    @pl.loop(0, held.shape[0] // 32)
    def _(i):
        at = pl.ds(pl.multiple_of(i * 32, 32), 32)
        held[at, :] = normalized(held[at, :], gain_ref[...])[2]

    for i, group in enumerate(zip(*loads)):
        at = slice(i * CHUNK, (i + 1) * CHUNK)
        for load, w, total in zip(group, (wq, wk, wv), (tq, tk, tv)):
            load.wait()
            product = dot_nn(held[:, at], w[at, :])
            total[...] = product if i == 0 else total[...] + product
    tokens, width = tq.shape
    seen = seen_pairs(blocks_ref, counts_ref, tokens)
    for h in range(width // HD):
        cols = slice(h * HD, (h + 1) * HD)
        query, key, value = (t[:, cols].astype(BF16) for t in (tq, tk, tv))
        soft = soft_scores(query, key, factor_ref[0, h], seen)
        att[:, cols] = dot_nn(soft.astype(BF16), value).astype(BF16)
    load_wo.wait()
    for i in range(wo.shape[1] // CHUNK):
        at = slice(i * CHUNK, (i + 1) * CHUNK)
        held[:, at] = dot_nn(att[...], wo[:, at]).astype(BF16)
        split_rows(held, near_ref, far_ref, 1, 2, at, at)


def forward_terms(blocks, counts, factor, xs, gain, wq, wk, wv, wo, after=()):
    n = len(xs)
    _, rows, model = xs[0].shape
    width = wq.shape[1]
    tokens = 4 * rows
    return pl.pallas_call(
        functools.partial(forward_kernel, n, len(after)),
        out_shape=(sds((2, rows, model), BF16),) * 2,
        in_specs=[SMEM] * 3 + [HBM] * n + [VMEM] + [HBM] * (4 + len(after)),
        scratch_shapes=[pltpu.VMEM((tokens, model), BF16)]
        + [pltpu.VMEM(wq.shape, BF16)] * 3
        + [pltpu.VMEM(wo.shape, BF16)]
        + [pltpu.VMEM((tokens, width), F32)] * 3
        + [
            pltpu.VMEM((tokens, width), BF16),
            pltpu.SemaphoreType.DMA((n + 1,)),
            pltpu.SemaphoreType.DMA((3, model // CHUNK)),
        ],
        compiler_params=params(),
        cost_estimate=SMALL,
        name="forward_terms",
    )(blocks, counts, factor, *xs, gain, wq, wk, wv, wo, *after)


def back_kernel(near_ref, came_ref, last_ref, x_ref, ins_ref, gain_ref, *rest):
    back_ref, part_ref = rest[-2:]
    gain = gain_ref[...]
    unit, inverse, _ = normalized(x_ref[...], gain)
    grad = near_ref[0].astype(F32) + came_ref[0].astype(F32) + last_ref[...].astype(F32)
    scaled = gain * grad
    part_ref[...] = jnp.sum(grad * unit, axis=0, keepdims=True)
    inner = jnp.mean(scaled * unit, axis=-1, keepdims=True)
    back_ref[...] = (ins_ref[0].astype(F32) + inverse * (scaled - unit * inner)).astype(BF16)


def back(near, came, last, x, ins, gain, after=()):
    return pl.pallas_call(
        back_kernel,
        out_shape=(sds(x.shape, BF16), sds(gain.shape, F32)),
        in_specs=[VMEM] * 6 + [HBM] * len(after),
        compiler_params=params(),
        cost_estimate=SMALL,
        name="back",
    )(near, came, last, x, ins, gain, *after)


def slice_copies(which, parts, cols, sems):
    seq, dp = lax.axis_index("seq"), lax.axis_index("dp")
    copies = []
    for j, part in enumerate(parts):
        _, n, rows, _ = part.shape
        at = pl.ds(pl.multiple_of((seq ^ j) * rows, rows), rows)
        for k in range(n):
            sample = lax.rem(dp + n - k, n)
            source = part.at[which, k]
            copies.append(pltpu.make_async_copy(source, cols.at[sample, at], sems.at[j, k]))
    return copies


def weight_kernel(n_seq, n_dp, *rest):
    parts, own, rest = rest[:n_seq], rest[n_seq], rest[n_seq + 1 :]
    lower, upper = rest[: n_dp - 1], rest[n_dp - 1 : 2 * n_dp - 2]
    out_q, out_k, out_v, cols, grads, sems, own_sems = rest[-7:]
    me = lax.axis_index("dp")

    def grad_copies(act):
        act(pltpu.make_async_copy(own, grads.at[me], own_sems.at[0]))
        for k in range(1, n_dp):
            spot = grads.at[lax.rem(me + n_dp - k, n_dp)]

            @pl.when(me >= k)
            def _():
                act(pltpu.make_async_copy(lower[k - 1], spot, own_sems.at[k]))

            @pl.when(me < k)
            def _():
                act(pltpu.make_async_copy(upper[n_dp - k - 1], spot, own_sems.at[k]))

    grad_copies(lambda copy: copy.start())
    run_copies(slice_copies(0, parts, cols, sems))
    grad_copies(lambda copy: copy.wait())
    width = out_q.shape[1]
    tile = min(256, out_q.shape[0])
    samples, tokens, _ = cols.shape

    @pl.loop(0, out_q.shape[0] // tile)
    def _(i):
        at = pl.ds(pl.multiple_of(i * tile, tile), tile)
        total = dot_tn(
            cols[:, :, at].reshape(samples * tokens, tile),
            grads[...].reshape(samples * tokens, 3 * width),
        ).astype(BF16)
        for o, out in enumerate((out_q, out_k, out_v)):
            out[at, :] = total[:, o * width : (o + 1) * width]


def out_weight_kernel(n_seq, n_dp, *rest):
    parts, factors_in = rest[:n_seq], rest[n_seq : n_seq + n_dp]
    out_ref, cols, factors, sems, own_sems = rest[-5:]
    dp = lax.axis_index("dp")
    copies = slice_copies(1, parts, cols, sems)
    for k, source in enumerate(factors_in):
        spot = factors.at[lax.rem(dp + n_dp - k, n_dp)]
        copies.append(pltpu.make_async_copy(source, spot, own_sems.at[k]))
    run_copies(copies)
    samples, tokens, slice_width = cols.shape
    tile = 128

    @pl.loop(0, out_ref.shape[0] // tile)
    def _(i):
        at = pl.ds(pl.multiple_of(i * tile, tile), tile)
        out_ref[at, :] = dot_tn(
            factors[:, :, at].reshape(samples * tokens, tile),
            cols[...].reshape(samples * tokens, slice_width),
        ).astype(BF16)


def contracted(kernel, name, parts, factors, out_shape, after=()):
    _, samples, rows, slice_width = parts[0].shape
    tokens, width = factors[0].shape
    return pl.pallas_call(
        functools.partial(kernel, len(parts), samples),
        out_shape=out_shape,
        in_specs=[HBM] * (len(parts) + len(factors) + len(after)),
        scratch_shapes=[
            pltpu.VMEM((samples, len(parts) * rows, slice_width), BF16),
            pltpu.VMEM((samples, tokens, width), BF16),
            pltpu.SemaphoreType.DMA((len(parts), samples)),
            pltpu.SemaphoreType.DMA((samples,)),
        ],
        compiler_params=params(),
        cost_estimate=SMALL,
        name=name,
    )(*parts, *factors, *after)


def weight_grads(parts, own, lower, upper):
    shape = sds((parts[0].shape[3], own.shape[1] // 3), BF16)
    return contracted(weight_kernel, "weight_grads", parts, [own, *lower, *upper], (shape,) * 3)


def out_weight_grads(parts, atts, after=()):
    shape = sds((atts[0].shape[1], parts[0].shape[3]), BF16)
    return contracted(out_weight_kernel, "out_weight_grads", parts, atts, shape, after)


def half_relay_kernel(first_ref, second_ref, *rest):
    for_x, for_y = rest[-2:]
    half = for_x.shape[1]
    for_x[...] = second_ref[:, :half]
    for_y[...] = first_ref[:, half:]


def half_relayed(first, second, after=()):
    pair, rows, model = first.shape
    for_x, for_y = pl.pallas_call(
        half_relay_kernel,
        out_shape=(sds((pair, rows // 2, model), BF16),) * 2,
        in_specs=[VMEM] * 2 + [HBM] * len(after),
        compiler_params=params(),
        cost_estimate=SMALL,
        name="half_relay",
    )(first, second, *after)
    return [swapped(for_x, "seq", 1), swapped(for_y, "seq", 2)], for_x


def stack_kernel(n, *rest):
    out_ref = rest[-1]
    for k in range(n):
        out_ref[:, k] = rest[k][...]


def stacked(parts, after=()):
    n = len(parts)
    pair, rows, width = parts[0].shape
    return pl.pallas_call(
        functools.partial(stack_kernel, n),
        out_shape=sds((pair, n, rows, width), BF16),
        in_specs=[VMEM] * n + [HBM] * len(after),
        compiler_params=params(),
        cost_estimate=SMALL,
        name="stack",
    )(*parts, *after)


def add_kernel(near_ref, came_ref, *rest):
    rest[-1][...] = (near_ref[1].astype(F32) + came_ref[1].astype(F32)).astype(BF16)


def added(near, came, after=()):
    return pl.pallas_call(
        add_kernel,
        out_shape=sds(near.shape[1:], BF16),
        in_specs=[VMEM] * 2 + [HBM] * len(after),
        compiler_params=params(),
        cost_estimate=SMALL,
        name="add",
    )(near, came, *after)


def swapped(value, axis, j):
    return lax.ppermute(value, axis, [(i, i ^ j) for i in range(lax.axis_size(axis))])


def crossed(value, j):
    n = lax.axis_size("seq")
    pairs = [(p * n + i, (1 - p) * n + (i ^ j)) for p in range(2) for i in range(n)]
    return lax.ppermute(value, ("pipe", "seq"), pairs)


def rotated(value, axis, k):
    n = lax.axis_size(axis)
    return lax.ppermute(value, axis, [(i, (i + k) % n) for i in range(n)])


def shifted(value, axis, by):
    n = lax.axis_size(axis)
    return lax.ppermute(value, axis, [(i, i + by) for i in range(n) if 0 <= i + by < n])


def line_gathered(value, axis):
    lower, upper, up, down = [], [], value, value
    for _ in range(lax.axis_size(axis) - 1):
        up, down = shifted(up, axis, 1), shifted(down, axis, -1)
        lower.append(up)
        upper.append(down)
    return lower, upper


def exchanged(parts, axis):
    return [parts[0]] + [rotated(parts[k], axis, k) for k in range(1, len(parts))]


def summed(value, axis):
    hop = 1
    while hop < lax.axis_size(axis):
        value, hop = value + swapped(value, axis, hop), 2 * hop
    return value


def local(
    encoded,
    sent_forward,
    head_cotangent,
    grad_sent,
    x_saved,
    q_saved,
    k_saved,
    v_saved,
    norm_gain,
    logit_scale,
    w_query,
    w_key,
    w_value,
    w_out,
    key_blocks,
    key_counts,
):
    n_dp = lax.axis_size("dp")
    factor = logit_scale / math.sqrt(HD)
    blocks, counts = key_blocks[0], key_counts[0]
    wq, wk, wv, wo = w_query[0], w_key[0], w_value[0], w_out[0]
    q, k, v, x = q_saved[0, 0], k_saved[0, 0], v_saved[0, 0], x_saved[0, 0]

    sent = pick(sent_forward[0, 0], encoded[0], grad_sent[0, 0], head_cotangent[0])
    ins = [crossed(sent, j) for j in range(3)]
    column_sets = column_parts(x, ins[0], norm_gain, n_dp)
    moved = exchanged(column_sets, "dp")
    soft, att = saved_attention(blocks, counts, factor, q, k, v, after=column_sets[:1])
    halves, token = half_relayed(ins[1], ins[2], after=[att, *moved[1:]])
    ins = ins + halves
    atts = exchanged([att] * n_dp, "dp")
    cols = stacked(moved, after=halves + atts[1::2])
    cols = [cols] + [swapped(cols, "seq", j) for j in (1, 2)]

    grads = backward_attention(factor, ins, wo, soft, att, q, k, v, after=[cols[0]])
    lower, upper = line_gathered(grads, "dp")
    dx_near, dx_far = input_grads(grads, wq, wk, wv, after=cols[1:])
    dx_came = swapped(dx_far, "seq", 1)
    cols = cols + [swapped(cols[1], "seq", 2)]
    mix_near, mix_far = forward_terms(
        blocks,
        counts,
        factor,
        ins,
        norm_gain,
        wq,
        wk,
        wv,
        wo,
        after=[dx_near, *cols[1:3], *lower[:1], *upper[:1]],
    )
    mix_came = swapped(mix_far, "seq", 1)
    dx_sum = added(dx_near, dx_came, after=[mix_near])
    dx_last = swapped(dx_sum, "seq", 2)
    grad_out = out_weight_grads(cols, atts, after=[dx_sum, *lower[1:2], *upper[1:2]])
    back_out, gain_part = back(dx_near, dx_came, dx_last, x, ins[0], norm_gain, after=[grad_out])
    mix_sum = added(mix_near, mix_came, after=[back_out, *lower[2:3], *upper[2:3]])
    mix_last = swapped(mix_sum, "seq", 2)

    gain_part = summed(summed(gain_part, "seq"), "dp")
    total = mix_near[0].astype(F32) + mix_came[0].astype(F32) + mix_last.astype(F32)
    forward_out = (ins[0][1].astype(F32) + total).astype(BF16)

    grad_q, grad_k, grad_v = weight_grads(cols, grads, lower, upper)
    return (
        forward_out[None, None],
        back_out[None, None],
        grad_q[None],
        grad_k[None],
        grad_v[None],
        grad_out[None],
        gain_part,
    )


def solution(mesh):
    in_specs = (
        P("dp", "seq", None),
        P("pipe", "dp", "seq", None),
        P("dp", "seq", None),
        P("pipe", "dp", "seq", None),
        P("pipe", "dp", "seq", None),
        P("pipe", "dp", None, "seq"),
        P("pipe", "dp", None, "seq"),
        P("pipe", "dp", None, "seq"),
        P("pipe", None),
        P("pipe", "seq"),
        P("pipe", None, "seq"),
        P("pipe", None, "seq"),
        P("pipe", None, "seq"),
        P("pipe", "seq", None),
        P("dp", None, None),
        P("dp", None),
    )
    out_specs = (
        P("pipe", "dp", "seq", None),
        P("pipe", "dp", "seq", None),
        P("pipe", "dp", "seq"),
        P("pipe", "dp", "seq"),
        P("pipe", "dp", "seq"),
        P("pipe", "seq", "dp"),
        P("pipe", None),
    )
    return jax.shard_map(local, mesh=mesh, in_specs=in_specs, out_specs=out_specs, check_vma=False)
```

```python
import functools
import math

import jax
import jax.numpy as jnp
from jax import lax
from jax.experimental import pallas as pl
from jax.experimental.pallas import tpu as pltpu
from jax.sharding import PartitionSpec as P

HD = 128
BLOCK = 128
EPSILON = 1e-05
CHUNK = 512
MIB = 1024 * 1024

BF16 = jnp.bfloat16
F32 = jnp.float32
HBM = pl.BlockSpec(memory_space=pl.ANY)
VMEM = pl.BlockSpec(memory_space=pltpu.VMEM)
SMEM = pl.BlockSpec(memory_space=pltpu.SMEM)


def dot_nn(a, b):
    return lax.dot_general(a, b, (((1,), (0,)), ((), ())), preferred_element_type=F32)


def dot_nt(a, b):
    return lax.dot_general(a, b, (((1,), (1,)), ((), ())), preferred_element_type=F32)


def dot_tn(a, b):
    return lax.dot_general(a, b, (((0,), (0,)), ((), ())), preferred_element_type=F32)


def sds(shape, dtype):
    return jax.ShapeDtypeStruct(shape, dtype)


def params(grid=0):
    semantics = ("arbitrary",) * grid if grid else None
    return pltpu.CompilerParams(vmem_limit_bytes=64 * MIB, dimension_semantics=semantics)


SMALL = pl.CostEstimate(flops=1024, bytes_accessed=1024, transcendentals=0)


def run_copies(copies):
    for copy in copies:
        copy.start()
    for copy in copies:
        copy.wait()


def normalized(rows, gain):
    widened = rows.astype(F32)
    inverse = lax.rsqrt(jnp.mean(widened * widened, axis=-1, keepdims=True) + EPSILON)
    unit = widened * inverse
    return unit, inverse, (unit * gain).astype(BF16)


def seen_pairs(blocks_ref, counts_ref, tokens):
    count, slots = blocks_ref.shape
    row_block = lax.broadcasted_iota(jnp.int32, (tokens, tokens), 0) // BLOCK
    col_block = lax.broadcasted_iota(jnp.int32, (tokens, tokens), 1) // BLOCK
    seen = jnp.zeros((tokens, tokens), jnp.int32)
    for i in range(count):
        for j in range(count):
            flag = jnp.int32(0)
            for t in range(slots):
                listed = (t < counts_ref[i]) & (blocks_ref[i, t] == j)
                flag = flag | listed.astype(jnp.int32)
            seen = jnp.where((row_block == i) & (col_block == j), flag, seen)
    return seen


def soft_scores(query, key, factor, seen):
    scores = dot_nt(query, key) * factor
    scores = jnp.where(seen > 0, scores, -1e30)
    lifted = jnp.exp(scores - jnp.max(scores, axis=-1, keepdims=True))
    return lifted / jnp.sum(lifted, axis=-1, keepdims=True)


def pick_kernel(forward_ref, encoded_ref, grad_ref, head_ref, out_ref, sems):
    section = lax.axis_index("pipe")

    def both(first, second):
        run_copies(
            [
                pltpu.make_async_copy(first, out_ref.at[0], sems.at[0]),
                pltpu.make_async_copy(second, out_ref.at[1], sems.at[1]),
            ]
        )

    @pl.when(section == 0)
    def _():
        both(head_ref, forward_ref)

    @pl.when(section != 0)
    def _():
        both(grad_ref, encoded_ref)


def pick(sent_forward, encoded, grad_sent, head):
    return pl.pallas_call(
        pick_kernel,
        out_shape=sds((2,) + encoded.shape, BF16),
        in_specs=[HBM] * 4,
        scratch_shapes=[pltpu.SemaphoreType.DMA((2,))],
        compiler_params=params(),
        cost_estimate=SMALL,
        name="pick",
    )(sent_forward, encoded, grad_sent, head)


def columns_kernel(x_ref, ins_ref, gain_ref, *rest):
    outs, held = rest[:-1], rest[-1]
    me = lax.axis_index("dp")
    n = len(outs)
    width = outs[0].shape[-1]
    held[...] = normalized(x_ref[...], gain_ref[...])[2]
    for k, out in enumerate(outs):
        start = pl.multiple_of(lax.rem(me + k, n) * width, width)
        out[0] = held[:, pl.ds(start, width)]
        out[1] = ins_ref[0, :, pl.ds(start, width)]


def column_parts(x, ins, gain, n):
    rows, width = x.shape
    part = (2, rows, width // n)
    return pl.pallas_call(
        columns_kernel,
        out_shape=tuple(sds(part, BF16) for _ in range(n)),
        scratch_shapes=[pltpu.VMEM((rows, width), BF16)],
        compiler_params=params(),
        cost_estimate=SMALL,
        name="columns",
    )(x, ins, gain)


def saved_kernel(blocks_ref, counts_ref, factor_ref, q_ref, k_ref, v_ref, *rest):
    soft_ref, att_ref = rest[-2:]
    tokens, width = q_ref.shape
    seen = seen_pairs(blocks_ref, counts_ref, tokens)
    for h in range(width // HD):
        cols = slice(h * HD, (h + 1) * HD)
        soft = soft_scores(q_ref[:, cols], k_ref[:, cols], factor_ref[0, h], seen)
        soft_ref[h] = soft
        att_ref[:, cols] = dot_nn(soft.astype(BF16), v_ref[:, cols]).astype(BF16)


def saved_attention(blocks, counts, factor, q, k, v, after=()):
    tokens, width = q.shape
    heads = width // HD
    return pl.pallas_call(
        saved_kernel,
        out_shape=(sds((heads, tokens, tokens), F32), sds((tokens, width), BF16)),
        in_specs=[SMEM] * 3 + [VMEM] * 3 + [HBM] * len(after),
        compiler_params=params(),
        cost_estimate=SMALL,
        name="saved_attention",
    )(blocks, counts, factor, q, k, v, *after)


def placed(refs, which):
    return [ref.at[which] for ref in refs[:3]] + [refs[3]]


def block_copies(refs, which, held, sems):
    me = lax.axis_index("seq")
    rows = refs[0].shape[1]
    copies = []
    for j, ref in enumerate(refs):
        at = (me ^ min(j, 3)) * rows + (rows // 2 if j == 4 else 0)
        spot = held.at[pl.ds(pl.multiple_of(at, rows // 2), ref.shape[1])]
        copies.append(pltpu.make_async_copy(ref.at[which], spot, sems.at[j]))
    return copies


def split_rows(held, near_ref, far_ref, first, second, cols_in, cols_out):
    me = lax.axis_index("seq")
    rows = near_ref.shape[1]
    for ref, hop in ((near_ref, 0), (far_ref, first)):
        for i, other in enumerate((0, second)):
            at = pl.multiple_of((me ^ hop ^ other) * rows, rows)
            ref[i, :, cols_out] = held[pl.ds(at, rows), cols_in]


LOADS = 8


def chunk_loads(source, held, sems):
    rows = source.shape[0] // LOADS
    return [
        pltpu.make_async_copy(
            source.at[pl.ds(i * rows, rows)], held.at[pl.ds(i * rows, rows)], sems.at[i]
        )
        for i in range(LOADS)
    ]


def start_all(copies):
    for copy in copies:
        copy.start()


def wait_all(copies):
    for copy in copies:
        copy.wait()


def backward_kernel(n, factor_ref, *rest):
    cots, rest = rest[:n], rest[n:]
    soft_in, source, att_ref, q_ref, k_ref, v_ref = rest[:6]
    out_ref, held, soft_ref, low, wo, sems, soft_sem, w_sems = rest[-8:]
    width = q_ref.shape[1]
    copies = block_copies(cots, 0, held, sems)
    loads = chunk_loads(source, wo, w_sems)
    load_soft = pltpu.make_async_copy(soft_in, soft_ref, soft_sem.at[0])
    start_all(copies)
    start_all(loads)
    wait_all(copies)
    load_soft.start()
    wait_all(loads)
    low[...] = dot_nt(held[...], wo[...]).astype(BF16)
    load_soft.wait()
    for h in range(width // HD):
        cols = slice(h * HD, (h + 1) * HD)
        cot = low[:, cols]
        soft = soft_ref[h]
        products = cot.astype(F32) * att_ref[:, cols].astype(F32)
        dots = jnp.sum(products, axis=-1, keepdims=True)
        grads = soft * (dot_nt(cot, v_ref[:, cols]) - dots) * factor_ref[0, h]
        grads = grads.astype(BF16)
        soft = soft.astype(BF16)
        out_ref[:, h * HD : (h + 1) * HD] = dot_nn(grads, k_ref[:, cols]).astype(BF16)
        key_at = width + h * HD
        out_ref[:, key_at : key_at + HD] = dot_tn(grads, q_ref[:, cols]).astype(BF16)
        value_at = 2 * width + h * HD
        out_ref[:, value_at : value_at + HD] = dot_tn(soft, cot).astype(BF16)


def backward_attention(factor, cots, soft, wo, att, q, k, v, after=()):
    tokens, width = q.shape
    n = len(cots)
    return pl.pallas_call(
        functools.partial(backward_kernel, n),
        out_shape=sds((tokens, 3 * width), BF16),
        in_specs=[SMEM] + [HBM] * (n + 2) + [VMEM] * 4 + [HBM] * len(after),
        scratch_shapes=[
            pltpu.VMEM((tokens, wo.shape[1]), BF16),
            pltpu.VMEM(soft.shape, F32),
            pltpu.VMEM((tokens, width), BF16),
            pltpu.VMEM(wo.shape, BF16),
            pltpu.SemaphoreType.DMA((n,)),
            pltpu.SemaphoreType.DMA((1,)),
            pltpu.SemaphoreType.DMA((LOADS,)),
        ],
        compiler_params=params(),
        cost_estimate=SMALL,
        name="backward_attention",
    )(factor, *cots, soft, wo, att, q, k, v, *after)


def input_grad_kernel(g_ref, *rest):
    near_ref, far_ref, tile, wq, wk, wv, sems = rest[-7:]
    rows, width = wq.shape[0] // LOADS, wq.shape[1]
    groups = list(
        zip(*(chunk_loads(rest[i], w, sems.at[i]) for i, w in enumerate((wq, wk, wv))))
    )
    for group in groups[:3]:
        start_all(group)
    for i, group in enumerate(groups):
        wait_all(group)
        if i + 3 < LOADS:
            start_all(groups[i + 3])
        at = slice(i * rows, (i + 1) * rows)
        total = dot_nt(g_ref[:, :width], wq[at, :])
        total += dot_nt(g_ref[:, width : 2 * width], wk[at, :])
        total += dot_nt(g_ref[:, 2 * width :], wv[at, :])
        tile[...] = total.astype(BF16)
        split_rows(tile, near_ref, far_ref, 1, 2, slice(None), at)


def input_grads(grads, wq, wk, wv, after=()):
    tokens = grads.shape[0]
    model = wq.shape[0]
    return pl.pallas_call(
        input_grad_kernel,
        out_shape=(sds((2, tokens // 4, model), BF16),) * 2,
        in_specs=[VMEM] + [HBM] * (3 + len(after)),
        scratch_shapes=[pltpu.VMEM((tokens, model // LOADS), BF16)]
        + [pltpu.VMEM(wq.shape, BF16)] * 3
        + [pltpu.SemaphoreType.DMA((3, LOADS))],
        compiler_params=params(),
        cost_estimate=SMALL,
        name="input_grads",
    )(grads, wq, wk, wv, *after)


def forward_kernel(n, blocks_ref, counts_ref, factor_ref, *rest):
    xs, rest = rest[:n], rest[n:]
    gain_ref, sources = rest[0], rest[1:5]
    near_ref, far_ref, held, low, att, wq, wk, wv, wo, sems, w_sems = rest[-11:]
    copies = block_copies(xs, 1, held, sems)
    loads = [
        chunk_loads(source, w, w_sems.at[i])
        for i, (source, w) in enumerate(zip(sources, (wq, wk, wv, wo)))
    ]
    start_all(copies)
    start_all(loads[0])
    wait_all(copies)
    tokens = held.shape[0]
    width = wq.shape[1]

    @pl.loop(0, tokens // 32)
    def _(i):
        at = pl.ds(pl.multiple_of(i * 32, 32), 32)
        held[at, :] = normalized(held[at, :], gain_ref[...])[2]

    for i, w in enumerate((wq, wk, wv)):
        start_all(loads[i + 1])
        wait_all(loads[i])
        low[:, i * width : (i + 1) * width] = dot_nn(held[...], w[...]).astype(BF16)
    seen = seen_pairs(blocks_ref, counts_ref, tokens)
    for h in range(width // HD):
        query, key, value = (
            low[:, i * width + h * HD : i * width + (h + 1) * HD] for i in range(3)
        )
        soft = soft_scores(query, key, factor_ref[0, h], seen)
        att[:, h * HD : (h + 1) * HD] = dot_nn(soft.astype(BF16), value).astype(BF16)
    wait_all(loads[3])
    for i in range(wo.shape[1] // CHUNK):
        at = slice(i * CHUNK, (i + 1) * CHUNK)
        held[:, at] = dot_nn(att[...], wo[:, at]).astype(BF16)
        split_rows(held, near_ref, far_ref, 1, 2, at, at)


def forward_terms(blocks, counts, factor, xs, gain, weights, after=()):
    n = len(xs)
    _, rows, model = xs[0].shape
    width = weights[0].shape[1]
    tokens = 4 * rows
    return pl.pallas_call(
        functools.partial(forward_kernel, n),
        out_shape=(sds((2, rows, model), BF16),) * 2,
        in_specs=[SMEM] * 3 + [HBM] * n + [VMEM] + [HBM] * (4 + len(after)),
        scratch_shapes=[
            pltpu.VMEM((tokens, model), BF16),
            pltpu.VMEM((tokens, 3 * width), BF16),
            pltpu.VMEM((tokens, width), BF16),
        ]
        + [pltpu.VMEM(w.shape, BF16) for w in weights]
        + [pltpu.SemaphoreType.DMA((n,)), pltpu.SemaphoreType.DMA((4, LOADS))],
        compiler_params=params(),
        cost_estimate=SMALL,
        name="forward_terms",
    )(blocks, counts, factor, *xs, gain, *weights, *after)


def back_kernel(near_ref, came_ref, last_ref, x_ref, ins_ref, gain_ref, *rest):
    back_ref, part_ref = rest[-2:]
    gain = gain_ref[...]
    unit, inverse, _ = normalized(x_ref[...], gain)
    grad = near_ref[0].astype(F32) + came_ref[0].astype(F32) + last_ref[...].astype(F32)
    scaled = gain * grad
    part_ref[...] = jnp.sum(grad * unit, axis=0, keepdims=True)
    inner = jnp.mean(scaled * unit, axis=-1, keepdims=True)
    back_ref[...] = (ins_ref[0].astype(F32) + inverse * (scaled - unit * inner)).astype(BF16)


def back(near, came, last, x, ins, gain, after=()):
    return pl.pallas_call(
        back_kernel,
        out_shape=(sds(x.shape, BF16), sds(gain.shape, F32)),
        in_specs=[VMEM] * 6 + [HBM] * len(after),
        compiler_params=params(),
        cost_estimate=SMALL,
        name="back",
    )(near, came, last, x, ins, gain, *after)


def slice_copies(which, parts, cols, sems):
    seq, dp = lax.axis_index("seq"), lax.axis_index("dp")
    copies = []
    for j, part in enumerate(parts):
        _, n, rows, _ = part.shape
        at = pl.ds(pl.multiple_of((seq ^ j) * rows, rows), rows)
        for k in range(n):
            sample = lax.rem(dp + n - k, n)
            source = part.at[which, k]
            copies.append(pltpu.make_async_copy(source, cols.at[sample, at], sems.at[j, k]))
    return copies


def weight_kernel(n_seq, n_dp, *rest):
    parts, own, rest = rest[:n_seq], rest[n_seq], rest[n_seq + 1 :]
    lower, upper = rest[: n_dp - 1], rest[n_dp - 1 : 2 * n_dp - 2]
    out_q, out_k, out_v, cols, grads, sems, own_sems = rest[-7:]
    me = lax.axis_index("dp")

    def grad_copies(act):
        act(pltpu.make_async_copy(own, grads.at[me], own_sems.at[0]))
        for k in range(1, n_dp):
            spot = grads.at[lax.rem(me + n_dp - k, n_dp)]

            @pl.when(me >= k)
            def _():
                act(pltpu.make_async_copy(lower[k - 1], spot, own_sems.at[k]))

            @pl.when(me < k)
            def _():
                act(pltpu.make_async_copy(upper[n_dp - k - 1], spot, own_sems.at[k]))

    grad_copies(lambda copy: copy.start())
    run_copies(slice_copies(0, parts, cols, sems))
    grad_copies(lambda copy: copy.wait())
    width = out_q.shape[1]
    tile = min(256, out_q.shape[0])
    samples, tokens, _ = cols.shape

    @pl.loop(0, out_q.shape[0] // tile)
    def _(i):
        at = pl.ds(pl.multiple_of(i * tile, tile), tile)
        total = dot_tn(
            cols[:, :, at].reshape(samples * tokens, tile),
            grads[...].reshape(samples * tokens, 3 * width),
        ).astype(BF16)
        for o, out in enumerate((out_q, out_k, out_v)):
            out[at, :] = total[:, o * width : (o + 1) * width]


def out_weight_kernel(n_seq, n_dp, *rest):
    parts, factors_in = rest[:n_seq], rest[n_seq : n_seq + n_dp]
    out_ref, cols, factors, sems, own_sems = rest[-5:]
    dp = lax.axis_index("dp")
    copies = slice_copies(1, parts, cols, sems)
    for k, source in enumerate(factors_in):
        spot = factors.at[lax.rem(dp + n_dp - k, n_dp)]
        copies.append(pltpu.make_async_copy(source, spot, own_sems.at[k]))
    run_copies(copies)
    samples, tokens, slice_width = cols.shape
    tile = 128

    @pl.loop(0, out_ref.shape[0] // tile)
    def _(i):
        at = pl.ds(pl.multiple_of(i * tile, tile), tile)
        out_ref[at, :] = dot_tn(
            factors[:, :, at].reshape(samples * tokens, tile),
            cols[...].reshape(samples * tokens, slice_width),
        ).astype(BF16)


def contracted(kernel, name, parts, factors, out_shape, after=()):
    _, samples, rows, slice_width = parts[0].shape
    tokens, width = factors[0].shape
    return pl.pallas_call(
        functools.partial(kernel, len(parts), samples),
        out_shape=out_shape,
        in_specs=[HBM] * (len(parts) + len(factors) + len(after)),
        scratch_shapes=[
            pltpu.VMEM((samples, len(parts) * rows, slice_width), BF16),
            pltpu.VMEM((samples, tokens, width), BF16),
            pltpu.SemaphoreType.DMA((len(parts), samples)),
            pltpu.SemaphoreType.DMA((samples,)),
        ],
        compiler_params=params(),
        cost_estimate=SMALL,
        name=name,
    )(*parts, *factors, *after)


def weight_grads(parts, own, lower, upper, after=()):
    shape = sds((parts[0].shape[3], own.shape[1] // 3), BF16)
    factors = [own, *lower, *upper]
    return contracted(weight_kernel, "weight_grads", parts, factors, (shape,) * 3, after)


def out_weight_grads(parts, atts, after=()):
    shape = sds((atts[0].shape[1], parts[0].shape[3]), BF16)
    return contracted(out_weight_kernel, "out_weight_grads", parts, atts, shape, after)


def half_relay_kernel(first_ref, second_ref, *rest):
    for_x, for_y, sems = rest[-3:]
    half = for_x.shape[1]
    run_copies(
        [
            pltpu.make_async_copy(second_ref.at[:, pl.ds(0, half)], for_x, sems.at[0]),
            pltpu.make_async_copy(first_ref.at[:, pl.ds(half, half)], for_y, sems.at[1]),
        ]
    )


def half_relayed(first, second, after=()):
    pair, rows, model = first.shape
    for_x, for_y = pl.pallas_call(
        half_relay_kernel,
        out_shape=(sds((pair, rows // 2, model), BF16),) * 2,
        in_specs=[HBM] * (2 + len(after)),
        scratch_shapes=[pltpu.SemaphoreType.DMA((2,))],
        compiler_params=params(),
        cost_estimate=SMALL,
        name="half_relay",
    )(first, second, *after)
    return [swapped(for_x, "seq", 1), swapped(for_y, "seq", 2)], for_x


def stack_kernel(n, *rest):
    out_ref, sems = rest[-2:]
    run_copies([pltpu.make_async_copy(rest[k], out_ref.at[:, k], sems.at[k]) for k in range(n)])


def stacked(parts, after=()):
    n = len(parts)
    pair, rows, width = parts[0].shape
    return pl.pallas_call(
        functools.partial(stack_kernel, n),
        out_shape=sds((pair, n, rows, width), BF16),
        in_specs=[HBM] * (n + len(after)),
        scratch_shapes=[pltpu.SemaphoreType.DMA((n,))],
        compiler_params=params(),
        cost_estimate=SMALL,
        name="stack",
    )(*parts, *after)


def add_kernel(near_ref, came_ref, *rest):
    out_ref, near, came, sems = rest[-4:]
    run_copies(
        [
            pltpu.make_async_copy(near_ref.at[1], near, sems.at[0]),
            pltpu.make_async_copy(came_ref.at[1], came, sems.at[1]),
        ]
    )
    out_ref[...] = (near[...].astype(F32) + came[...].astype(F32)).astype(BF16)


def added(near, came, after=()):
    shape = near.shape[1:]
    return pl.pallas_call(
        add_kernel,
        out_shape=sds(shape, BF16),
        in_specs=[HBM] * (2 + len(after)),
        scratch_shapes=[
            pltpu.VMEM(shape, BF16),
            pltpu.VMEM(shape, BF16),
            pltpu.SemaphoreType.DMA((2,)),
        ],
        compiler_params=params(),
        cost_estimate=SMALL,
        name="add",
    )(near, came, *after)


def passed_kernel(value_ref, *rest):
    out_ref, sems = rest[-2:]
    run_copies([pltpu.make_async_copy(value_ref, out_ref, sems.at[0])])


def passed(value, after):
    return pl.pallas_call(
        passed_kernel,
        out_shape=sds(value.shape, value.dtype),
        in_specs=[HBM] * (1 + len(after)),
        scratch_shapes=[pltpu.SemaphoreType.DMA((1,))],
        compiler_params=params(),
        cost_estimate=SMALL,
        name="passed",
    )(value, *after)


def gain_kernel(own_ref, came_ref, *rest):
    rest[-1][...] = own_ref[...] + came_ref[...]


def gain_added(own, came, after=()):
    return pl.pallas_call(
        gain_kernel,
        out_shape=sds(own.shape, F32),
        in_specs=[VMEM] * 2 + [HBM] * len(after),
        compiler_params=params(),
        cost_estimate=SMALL,
        name="gain_added",
    )(own, came, *after)


def swapped(value, axis, j):
    return lax.ppermute(value, axis, [(i, i ^ j) for i in range(lax.axis_size(axis))])


def crossed(value, j):
    n = lax.axis_size("seq")
    pairs = [(p * n + i, (1 - p) * n + (i ^ j)) for p in range(2) for i in range(n)]
    return lax.ppermute(value, ("pipe", "seq"), pairs)


def rotated(value, axis, k):
    n = lax.axis_size(axis)
    return lax.ppermute(value, axis, [(i, (i + k) % n) for i in range(n)])


def shifted(value, axis, by):
    n = lax.axis_size(axis)
    return lax.ppermute(value, axis, [(i, i + by) for i in range(n) if 0 <= i + by < n])


def line_gathered(value, axis):
    lower, upper, up, down = [], [], value, value
    for _ in range(lax.axis_size(axis) - 1):
        up, down = shifted(up, axis, 1), shifted(down, axis, -1)
        lower.append(up)
        upper.append(down)
    return lower, upper


def exchanged(parts, axis):
    return [parts[0]] + [rotated(parts[k], axis, k) for k in range(1, len(parts))]


def summed(value, axis):
    n = lax.axis_size(axis)
    if n <= 4:
        return sum((rotated(value, axis, k) for k in range(1, n)), value)
    hop = 1
    while hop < n:
        value, hop = value + swapped(value, axis, hop), 2 * hop
    return value


def local(
    encoded,
    sent_forward,
    head_cotangent,
    grad_sent,
    x_saved,
    q_saved,
    k_saved,
    v_saved,
    norm_gain,
    logit_scale,
    w_query,
    w_key,
    w_value,
    w_out,
    key_blocks,
    key_counts,
):
    n_dp = lax.axis_size("dp")
    factor = logit_scale / math.sqrt(HD)
    blocks, counts = key_blocks[0], key_counts[0]
    wq, wk, wv, wo = w_query[0], w_key[0], w_value[0], w_out[0]
    q, k, v, x = q_saved[0, 0], k_saved[0, 0], v_saved[0, 0], x_saved[0, 0]

    sent = pick(sent_forward[0, 0], encoded[0], grad_sent[0, 0], head_cotangent[0])
    ins = [crossed(sent, j) for j in range(3)]
    column_sets = column_parts(x, ins[0], norm_gain, n_dp)
    moved = exchanged(column_sets, "dp")
    soft, att = saved_attention(blocks, counts, factor, q, k, v, after=column_sets[:1])
    halves, token = half_relayed(ins[1], ins[2], after=[att, *moved[1:]])
    ins = ins + halves
    atts = exchanged([att] * n_dp, "dp")
    cols = stacked(moved, after=halves + atts[1:2])
    cols = [cols] + [swapped(cols, "seq", j) for j in (1, 2)]

    grads = backward_attention(factor, ins, soft, wo, att, q, k, v, after=[cols[0]])
    lower, upper = line_gathered(grads, "dp")
    dx_near, dx_far = input_grads(grads, wq, wk, wv)
    dx_far = passed(dx_far, after=cols[1:])
    dx_came = swapped(dx_far, "seq", 1)
    cols = cols + [swapped(cols[1], "seq", 2)]
    mix_near, mix_far = forward_terms(
        blocks,
        counts,
        factor,
        ins,
        norm_gain,
        (wq, wk, wv, wo),
        after=[dx_far, *lower[:1], *upper[:1]],
    )
    mix_came = swapped(mix_far, "seq", 1)
    dx_sum = added(dx_near, dx_came, after=[mix_near])
    dx_last = swapped(dx_sum, "seq", 2)
    back_out, gain_part = back(dx_near, dx_came, dx_last, x, ins[0], norm_gain, after=[cols[3], *lower[1:2], *upper[1:2]])
    mix_sum = added(mix_near, mix_came, after=[back_out, *lower[2:3], *upper[2:3]])
    mix_last = swapped(mix_sum, "seq", 2)

    gain_part = gain_added(gain_part, swapped(gain_part, "seq", 1), after=[mix_sum])
    gain_hop = swapped(gain_part, "seq", 2)
    grad_q, grad_k, grad_v = weight_grads(cols, grads, lower, upper, after=[gain_part])
    gain_part = gain_added(gain_part, gain_hop, after=[grad_q, mix_last])
    grad_out = out_weight_grads(cols, atts, after=[gain_part])
    gain_part = summed(gain_part, "dp")
    total = mix_near[0].astype(F32) + mix_came[0].astype(F32) + mix_last.astype(F32)
    forward_out = (ins[0][1].astype(F32) + total).astype(BF16)

    return (
        forward_out[None, None],
        back_out[None, None],
        grad_q[None],
        grad_k[None],
        grad_v[None],
        grad_out[None],
        gain_part,
    )


def solution(mesh):
    in_specs = (
        P("dp", "seq", None),
        P("pipe", "dp", "seq", None),
        P("dp", "seq", None),
        P("pipe", "dp", "seq", None),
        P("pipe", "dp", "seq", None),
        P("pipe", "dp", None, "seq"),
        P("pipe", "dp", None, "seq"),
        P("pipe", "dp", None, "seq"),
        P("pipe", None),
        P("pipe", "seq"),
        P("pipe", None, "seq"),
        P("pipe", None, "seq"),
        P("pipe", None, "seq"),
        P("pipe", "seq", None),
        P("dp", None, None),
        P("dp", None),
    )
    out_specs = (
        P("pipe", "dp", "seq", None),
        P("pipe", "dp", "seq", None),
        P("pipe", "dp", "seq"),
        P("pipe", "dp", "seq"),
        P("pipe", "dp", "seq"),
        P("pipe", "seq", "dp"),
        P("pipe", None),
    )
    return jax.shard_map(local, mesh=mesh, in_specs=in_specs, out_specs=out_specs, check_vma=False)
```

```python
import functools
import math

import jax
import jax.numpy as jnp
from jax import lax
from jax.experimental import pallas as pl
from jax.experimental.pallas import tpu as pltpu
from jax.sharding import PartitionSpec as P

HD = 128
BLOCK = 128
EPSILON = 1e-05
CHUNK = 512
MIB = 1024 * 1024

BF16 = jnp.bfloat16
F32 = jnp.float32
HBM = pl.BlockSpec(memory_space=pl.ANY)
VMEM = pl.BlockSpec(memory_space=pltpu.VMEM)
SMEM = pl.BlockSpec(memory_space=pltpu.SMEM)


def dot_nn(a, b):
    return lax.dot_general(a, b, (((1,), (0,)), ((), ())), preferred_element_type=F32)


def dot_nt(a, b):
    return lax.dot_general(a, b, (((1,), (1,)), ((), ())), preferred_element_type=F32)


def dot_tn(a, b):
    return lax.dot_general(a, b, (((0,), (0,)), ((), ())), preferred_element_type=F32)


def sds(shape, dtype):
    return jax.ShapeDtypeStruct(shape, dtype)


def params(grid=0):
    semantics = ("arbitrary",) * grid if grid else None
    return pltpu.CompilerParams(vmem_limit_bytes=64 * MIB, dimension_semantics=semantics)


SMALL = pl.CostEstimate(flops=1024, bytes_accessed=1024, transcendentals=0)


def run_copies(copies):
    for copy in copies:
        copy.start()
    for copy in copies:
        copy.wait()


def normalized(rows, gain):
    widened = rows.astype(F32)
    inverse = lax.rsqrt(jnp.mean(widened * widened, axis=-1, keepdims=True) + EPSILON)
    unit = widened * inverse
    return unit, inverse, (unit * gain).astype(BF16)


def seen_pairs(blocks_ref, counts_ref, tokens):
    count, slots = blocks_ref.shape
    row_block = lax.broadcasted_iota(jnp.int32, (tokens, tokens), 0) // BLOCK
    col_block = lax.broadcasted_iota(jnp.int32, (tokens, tokens), 1) // BLOCK
    seen = jnp.zeros((tokens, tokens), jnp.int32)
    for i in range(count):
        for j in range(count):
            flag = jnp.int32(0)
            for t in range(slots):
                listed = (t < counts_ref[i]) & (blocks_ref[i, t] == j)
                flag = flag | listed.astype(jnp.int32)
            seen = jnp.where((row_block == i) & (col_block == j), flag, seen)
    return seen


def soft_scores(query, key, factor, seen):
    scores = dot_nt(query, key) * factor
    scores = jnp.where(seen > 0, scores, -1e30)
    lifted = jnp.exp(scores - jnp.max(scores, axis=-1, keepdims=True))
    return lifted / jnp.sum(lifted, axis=-1, keepdims=True)


def pick_kernel(forward_ref, encoded_ref, grad_ref, head_ref, out_ref, sems):
    section = lax.axis_index("pipe")

    def both(first, second):
        run_copies(
            [
                pltpu.make_async_copy(first, out_ref.at[0], sems.at[0]),
                pltpu.make_async_copy(second, out_ref.at[1], sems.at[1]),
            ]
        )

    @pl.when(section == 0)
    def _():
        both(head_ref, forward_ref)

    @pl.when(section != 0)
    def _():
        both(grad_ref, encoded_ref)


def pick(sent_forward, encoded, grad_sent, head):
    return pl.pallas_call(
        pick_kernel,
        out_shape=sds((2,) + encoded.shape, BF16),
        in_specs=[HBM] * 4,
        scratch_shapes=[pltpu.SemaphoreType.DMA((2,))],
        compiler_params=params(),
        cost_estimate=SMALL,
        name="pick",
    )(sent_forward, encoded, grad_sent, head)


def columns_kernel(x_ref, ins_ref, gain_ref, *rest):
    outs, held = rest[:-1], rest[-1]
    me = lax.axis_index("dp")
    n = len(outs)
    width = outs[0].shape[-1]
    held[...] = normalized(x_ref[...], gain_ref[...])[2]
    for k, out in enumerate(outs):
        start = pl.multiple_of(lax.rem(me + k, n) * width, width)
        out[0] = held[:, pl.ds(start, width)]
        out[1] = ins_ref[0, :, pl.ds(start, width)]


def column_parts(x, ins, gain, n):
    rows, width = x.shape
    part = (2, rows, width // n)
    return pl.pallas_call(
        columns_kernel,
        out_shape=tuple(sds(part, BF16) for _ in range(n)),
        scratch_shapes=[pltpu.VMEM((rows, width), BF16)],
        compiler_params=params(),
        cost_estimate=SMALL,
        name="columns",
    )(x, ins, gain)


def saved_kernel(blocks_ref, counts_ref, factor_ref, q_ref, k_ref, v_ref, *rest):
    soft_ref, att_ref = rest[-2:]
    tokens, width = q_ref.shape
    seen = seen_pairs(blocks_ref, counts_ref, tokens)
    for h in range(width // HD):
        cols = slice(h * HD, (h + 1) * HD)
        soft = soft_scores(q_ref[:, cols], k_ref[:, cols], factor_ref[0, h], seen)
        soft_ref[h] = soft
        att_ref[:, cols] = dot_nn(soft.astype(BF16), v_ref[:, cols]).astype(BF16)


def saved_attention(blocks, counts, factor, q, k, v, after=()):
    tokens, width = q.shape
    heads = width // HD
    return pl.pallas_call(
        saved_kernel,
        out_shape=(sds((heads, tokens, tokens), F32), sds((tokens, width), BF16)),
        in_specs=[SMEM] * 3 + [VMEM] * 3 + [HBM] * len(after),
        compiler_params=params(),
        cost_estimate=SMALL,
        name="saved_attention",
    )(blocks, counts, factor, q, k, v, *after)


def placed(refs, which):
    return [ref.at[which] for ref in refs[:3]] + [refs[3]]


def block_copies(refs, which, held, sems):
    me = lax.axis_index("seq")
    rows = refs[0].shape[1]
    copies = []
    for j, ref in enumerate(refs):
        at = (me ^ min(j, 3)) * rows + (rows // 2 if j == 4 else 0)
        spot = held.at[pl.ds(pl.multiple_of(at, rows // 2), ref.shape[1])]
        copies.append(pltpu.make_async_copy(ref.at[which], spot, sems.at[j]))
    return copies


def split_rows(held, near_ref, far_ref, first, second, cols_in, cols_out):
    me = lax.axis_index("seq")
    rows = near_ref.shape[1]
    for ref, hop in ((near_ref, 0), (far_ref, first)):
        for i, other in enumerate((0, second)):
            at = pl.multiple_of((me ^ hop ^ other) * rows, rows)
            ref[i, :, cols_out] = held[pl.ds(at, rows), cols_in]


LOADS = 8


def chunk_loads(source, held, sems):
    rows = source.shape[0] // LOADS
    return [
        pltpu.make_async_copy(
            source.at[pl.ds(i * rows, rows)], held.at[pl.ds(i * rows, rows)], sems.at[i]
        )
        for i in range(LOADS)
    ]


def start_all(copies):
    for copy in copies:
        copy.start()


def wait_all(copies):
    for copy in copies:
        copy.wait()


def backward_kernel(n, factor_ref, *rest):
    cots, rest = rest[:n], rest[n:]
    soft_in, source, att_ref, q_ref, k_ref, v_ref = rest[:6]
    out_ref, held, soft_ref, low, wo, sems, soft_sem, w_sems = rest[-8:]
    width = q_ref.shape[1]
    copies = block_copies(cots, 0, held, sems)
    loads = chunk_loads(source, wo, w_sems)
    load_soft = pltpu.make_async_copy(soft_in, soft_ref, soft_sem.at[0])
    start_all(copies)
    start_all(loads)
    wait_all(copies)
    load_soft.start()
    wait_all(loads)
    low[...] = dot_nt(held[...], wo[...]).astype(BF16)
    load_soft.wait()
    for h in range(width // HD):
        cols = slice(h * HD, (h + 1) * HD)
        cot = low[:, cols]
        soft = soft_ref[h]
        products = cot.astype(F32) * att_ref[:, cols].astype(F32)
        dots = jnp.sum(products, axis=-1, keepdims=True)
        grads = soft * (dot_nt(cot, v_ref[:, cols]) - dots) * factor_ref[0, h]
        grads = grads.astype(BF16)
        soft = soft.astype(BF16)
        out_ref[:, h * HD : (h + 1) * HD] = dot_nn(grads, k_ref[:, cols]).astype(BF16)
        key_at = width + h * HD
        out_ref[:, key_at : key_at + HD] = dot_tn(grads, q_ref[:, cols]).astype(BF16)
        value_at = 2 * width + h * HD
        out_ref[:, value_at : value_at + HD] = dot_tn(soft, cot).astype(BF16)


def backward_attention(factor, cots, soft, wo, att, q, k, v, after=()):
    tokens, width = q.shape
    n = len(cots)
    return pl.pallas_call(
        functools.partial(backward_kernel, n),
        out_shape=sds((tokens, 3 * width), BF16),
        in_specs=[SMEM] + [HBM] * (n + 2) + [VMEM] * 4 + [HBM] * len(after),
        scratch_shapes=[
            pltpu.VMEM((tokens, wo.shape[1]), BF16),
            pltpu.VMEM(soft.shape, F32),
            pltpu.VMEM((tokens, width), BF16),
            pltpu.VMEM(wo.shape, BF16),
            pltpu.SemaphoreType.DMA((n,)),
            pltpu.SemaphoreType.DMA((1,)),
            pltpu.SemaphoreType.DMA((LOADS,)),
        ],
        compiler_params=params(),
        cost_estimate=SMALL,
        name="backward_attention",
    )(factor, *cots, soft, wo, att, q, k, v, *after)


def input_grad_kernel(g_ref, *rest):
    near_ref, far_ref, tile, wq, wk, wv, sems = rest[-7:]
    rows, width = wq.shape[0] // LOADS, wq.shape[1]
    groups = list(
        zip(*(chunk_loads(rest[i], w, sems.at[i]) for i, w in enumerate((wq, wk, wv))))
    )
    for group in groups[:3]:
        start_all(group)
    for i, group in enumerate(groups):
        wait_all(group)
        if i + 3 < LOADS:
            start_all(groups[i + 3])
        at = slice(i * rows, (i + 1) * rows)
        total = dot_nt(g_ref[:, :width], wq[at, :])
        total += dot_nt(g_ref[:, width : 2 * width], wk[at, :])
        total += dot_nt(g_ref[:, 2 * width :], wv[at, :])
        tile[...] = total.astype(BF16)
        split_rows(tile, near_ref, far_ref, 1, 2, slice(None), at)


def input_grads(grads, wq, wk, wv, after=()):
    tokens = grads.shape[0]
    model = wq.shape[0]
    return pl.pallas_call(
        input_grad_kernel,
        out_shape=(sds((2, tokens // 4, model), BF16),) * 2,
        in_specs=[VMEM] + [HBM] * (3 + len(after)),
        scratch_shapes=[pltpu.VMEM((tokens, model // LOADS), BF16)]
        + [pltpu.VMEM(wq.shape, BF16)] * 3
        + [pltpu.SemaphoreType.DMA((3, LOADS))],
        compiler_params=params(),
        cost_estimate=SMALL,
        name="input_grads",
    )(grads, wq, wk, wv, *after)


def forward_kernel(n, blocks_ref, counts_ref, factor_ref, *rest):
    xs, rest = rest[:n], rest[n:]
    gain_ref, sources = rest[0], rest[1:5]
    near_ref, far_ref, held, low, att, wq, wk, wv, wo, sems, w_sems = rest[-11:]
    copies = block_copies(xs, 1, held, sems)
    loads = [
        chunk_loads(source, w, w_sems.at[i])
        for i, (source, w) in enumerate(zip(sources, (wq, wk, wv, wo)))
    ]
    start_all(copies)
    start_all(loads[0])
    wait_all(copies)
    tokens = held.shape[0]
    width = wq.shape[1]

    @pl.loop(0, tokens // 32)
    def _(i):
        at = pl.ds(pl.multiple_of(i * 32, 32), 32)
        held[at, :] = normalized(held[at, :], gain_ref[...])[2]

    for i, w in enumerate((wq, wk, wv)):
        start_all(loads[i + 1])
        wait_all(loads[i])
        low[:, i * width : (i + 1) * width] = dot_nn(held[...], w[...]).astype(BF16)
    seen = seen_pairs(blocks_ref, counts_ref, tokens)
    for h in range(width // HD):
        query, key, value = (
            low[:, i * width + h * HD : i * width + (h + 1) * HD] for i in range(3)
        )
        soft = soft_scores(query, key, factor_ref[0, h], seen)
        att[:, h * HD : (h + 1) * HD] = dot_nn(soft.astype(BF16), value).astype(BF16)
    wait_all(loads[3])
    for i in range(wo.shape[1] // CHUNK):
        at = slice(i * CHUNK, (i + 1) * CHUNK)
        held[:, at] = dot_nn(att[...], wo[:, at]).astype(BF16)
        split_rows(held, near_ref, far_ref, 1, 2, at, at)


def forward_terms(blocks, counts, factor, xs, gain, weights, after=()):
    n = len(xs)
    _, rows, model = xs[0].shape
    width = weights[0].shape[1]
    tokens = 4 * rows
    return pl.pallas_call(
        functools.partial(forward_kernel, n),
        out_shape=(sds((2, rows, model), BF16),) * 2,
        in_specs=[SMEM] * 3 + [HBM] * n + [VMEM] + [HBM] * (4 + len(after)),
        scratch_shapes=[
            pltpu.VMEM((tokens, model), BF16),
            pltpu.VMEM((tokens, 3 * width), BF16),
            pltpu.VMEM((tokens, width), BF16),
        ]
        + [pltpu.VMEM(w.shape, BF16) for w in weights]
        + [pltpu.SemaphoreType.DMA((n,)), pltpu.SemaphoreType.DMA((4, LOADS))],
        compiler_params=params(),
        cost_estimate=SMALL,
        name="forward_terms",
    )(blocks, counts, factor, *xs, gain, *weights, *after)


def back_kernel(near_ref, came_ref, last_ref, x_ref, ins_ref, gain_ref, *rest):
    back_ref, part_ref = rest[-2:]
    gain = gain_ref[...]
    unit, inverse, _ = normalized(x_ref[...], gain)
    grad = near_ref[0].astype(F32) + came_ref[0].astype(F32) + last_ref[...].astype(F32)
    scaled = gain * grad
    part_ref[...] = jnp.sum(grad * unit, axis=0, keepdims=True)
    inner = jnp.mean(scaled * unit, axis=-1, keepdims=True)
    back_ref[...] = (ins_ref[0].astype(F32) + inverse * (scaled - unit * inner)).astype(BF16)


def back(near, came, last, x, ins, gain, after=()):
    return pl.pallas_call(
        back_kernel,
        out_shape=(sds(x.shape, BF16), sds(gain.shape, F32)),
        in_specs=[VMEM] * 6 + [HBM] * len(after),
        compiler_params=params(),
        cost_estimate=SMALL,
        name="back",
    )(near, came, last, x, ins, gain, *after)


def slice_copies(which, parts, cols, sems):
    seq, dp = lax.axis_index("seq"), lax.axis_index("dp")
    copies = []
    for j, part in enumerate(parts):
        _, n, rows, _ = part.shape
        at = pl.ds(pl.multiple_of((seq ^ j) * rows, rows), rows)
        for k in range(n):
            sample = lax.rem(dp + n - k, n)
            source = part.at[which, k]
            copies.append(pltpu.make_async_copy(source, cols.at[sample, at], sems.at[j, k]))
    return copies


def weight_kernel(n_seq, n_dp, *rest):
    parts, own, rest = rest[:n_seq], rest[n_seq], rest[n_seq + 1 :]
    lower, upper = rest[: n_dp - 1], rest[n_dp - 1 : 2 * n_dp - 2]
    out_q, out_k, out_v, cols, grads, sems, own_sems = rest[-7:]
    me = lax.axis_index("dp")

    def grad_copies(act):
        act(pltpu.make_async_copy(own, grads.at[me], own_sems.at[0]))
        for k in range(1, n_dp):
            spot = grads.at[lax.rem(me + n_dp - k, n_dp)]

            @pl.when(me >= k)
            def _():
                act(pltpu.make_async_copy(lower[k - 1], spot, own_sems.at[k]))

            @pl.when(me < k)
            def _():
                act(pltpu.make_async_copy(upper[n_dp - k - 1], spot, own_sems.at[k]))

    grad_copies(lambda copy: copy.start())
    run_copies(slice_copies(0, parts, cols, sems))
    grad_copies(lambda copy: copy.wait())
    width = out_q.shape[1]
    tile = min(512, out_q.shape[0])
    samples, tokens, _ = cols.shape

    @pl.loop(0, out_q.shape[0] // tile)
    def _(i):
        at = pl.ds(pl.multiple_of(i * tile, tile), tile)
        total = dot_tn(
            cols[:, :, at].reshape(samples * tokens, tile),
            grads[...].reshape(samples * tokens, 3 * width),
        ).astype(BF16)
        for o, out in enumerate((out_q, out_k, out_v)):
            out[at, :] = total[:, o * width : (o + 1) * width]


def out_weight_kernel(n_seq, n_dp, *rest):
    parts, factors_in = rest[:n_seq], rest[n_seq : n_seq + n_dp]
    out_ref, cols, factors, sems, own_sems = rest[-5:]
    dp = lax.axis_index("dp")
    copies = slice_copies(1, parts, cols, sems)
    for k, source in enumerate(factors_in):
        spot = factors.at[lax.rem(dp + n_dp - k, n_dp)]
        copies.append(pltpu.make_async_copy(source, spot, own_sems.at[k]))
    run_copies(copies)
    samples, tokens, slice_width = cols.shape
    tile = 512

    @pl.loop(0, out_ref.shape[0] // tile)
    def _(i):
        at = pl.ds(pl.multiple_of(i * tile, tile), tile)
        out_ref[at, :] = dot_tn(
            factors[:, :, at].reshape(samples * tokens, tile),
            cols[...].reshape(samples * tokens, slice_width),
        ).astype(BF16)


def contracted(kernel, name, parts, factors, out_shape, after=()):
    _, samples, rows, slice_width = parts[0].shape
    tokens, width = factors[0].shape
    return pl.pallas_call(
        functools.partial(kernel, len(parts), samples),
        out_shape=out_shape,
        in_specs=[HBM] * (len(parts) + len(factors) + len(after)),
        scratch_shapes=[
            pltpu.VMEM((samples, len(parts) * rows, slice_width), BF16),
            pltpu.VMEM((samples, tokens, width), BF16),
            pltpu.SemaphoreType.DMA((len(parts), samples)),
            pltpu.SemaphoreType.DMA((samples,)),
        ],
        compiler_params=params(),
        cost_estimate=SMALL,
        name=name,
    )(*parts, *factors, *after)


def weight_grads(parts, own, lower, upper, after=()):
    shape = sds((parts[0].shape[3], own.shape[1] // 3), BF16)
    factors = [own, *lower, *upper]
    return contracted(weight_kernel, "weight_grads", parts, factors, (shape,) * 3, after)


def out_weight_grads(parts, atts, after=()):
    shape = sds((atts[0].shape[1], parts[0].shape[3]), BF16)
    return contracted(out_weight_kernel, "out_weight_grads", parts, atts, shape, after)


def half_relay_kernel(first_ref, second_ref, *rest):
    for_x, for_y, sems = rest[-3:]
    half = for_x.shape[1]
    run_copies(
        [
            pltpu.make_async_copy(second_ref.at[:, pl.ds(0, half)], for_x, sems.at[0]),
            pltpu.make_async_copy(first_ref.at[:, pl.ds(half, half)], for_y, sems.at[1]),
        ]
    )


def half_relayed(first, second, after=()):
    pair, rows, model = first.shape
    for_x, for_y = pl.pallas_call(
        half_relay_kernel,
        out_shape=(sds((pair, rows // 2, model), BF16),) * 2,
        in_specs=[HBM] * (2 + len(after)),
        scratch_shapes=[pltpu.SemaphoreType.DMA((2,))],
        compiler_params=params(),
        cost_estimate=SMALL,
        name="half_relay",
    )(first, second, *after)
    return [swapped(for_x, "seq", 1), swapped(for_y, "seq", 2)], for_x


def stack_kernel(n, *rest):
    out_ref, sems = rest[-2:]
    run_copies([pltpu.make_async_copy(rest[k], out_ref.at[:, k], sems.at[k]) for k in range(n)])


def stacked(parts, after=()):
    n = len(parts)
    pair, rows, width = parts[0].shape
    return pl.pallas_call(
        functools.partial(stack_kernel, n),
        out_shape=sds((pair, n, rows, width), BF16),
        in_specs=[HBM] * (n + len(after)),
        scratch_shapes=[pltpu.SemaphoreType.DMA((n,))],
        compiler_params=params(),
        cost_estimate=SMALL,
        name="stack",
    )(*parts, *after)


def add_kernel(near_ref, came_ref, *rest):
    out_ref, near, came, sems = rest[-4:]
    run_copies(
        [
            pltpu.make_async_copy(near_ref.at[1], near, sems.at[0]),
            pltpu.make_async_copy(came_ref.at[1], came, sems.at[1]),
        ]
    )
    out_ref[...] = (near[...].astype(F32) + came[...].astype(F32)).astype(BF16)


def added(near, came, after=()):
    shape = near.shape[1:]
    return pl.pallas_call(
        add_kernel,
        out_shape=sds(shape, BF16),
        in_specs=[HBM] * (2 + len(after)),
        scratch_shapes=[
            pltpu.VMEM(shape, BF16),
            pltpu.VMEM(shape, BF16),
            pltpu.SemaphoreType.DMA((2,)),
        ],
        compiler_params=params(),
        cost_estimate=SMALL,
        name="add",
    )(near, came, *after)


def passed_kernel(value_ref, *rest):
    out_ref, sems = rest[-2:]
    run_copies([pltpu.make_async_copy(value_ref, out_ref, sems.at[0])])


def passed(value, after):
    return pl.pallas_call(
        passed_kernel,
        out_shape=sds(value.shape, value.dtype),
        in_specs=[HBM] * (1 + len(after)),
        scratch_shapes=[pltpu.SemaphoreType.DMA((1,))],
        compiler_params=params(),
        cost_estimate=SMALL,
        name="passed",
    )(value, *after)


def gain_kernel(own_ref, came_ref, *rest):
    rest[-1][...] = own_ref[...] + came_ref[...]


def gain_added(own, came, after=()):
    return pl.pallas_call(
        gain_kernel,
        out_shape=sds(own.shape, F32),
        in_specs=[VMEM] * 2 + [HBM] * len(after),
        compiler_params=params(),
        cost_estimate=SMALL,
        name="gain_added",
    )(own, came, *after)


def swapped(value, axis, j):
    return lax.ppermute(value, axis, [(i, i ^ j) for i in range(lax.axis_size(axis))])


def crossed(value, j):
    n = lax.axis_size("seq")
    pairs = [(p * n + i, (1 - p) * n + (i ^ j)) for p in range(2) for i in range(n)]
    return lax.ppermute(value, ("pipe", "seq"), pairs)


def rotated(value, axis, k):
    n = lax.axis_size(axis)
    return lax.ppermute(value, axis, [(i, (i + k) % n) for i in range(n)])


def shifted(value, axis, by):
    n = lax.axis_size(axis)
    return lax.ppermute(value, axis, [(i, i + by) for i in range(n) if 0 <= i + by < n])


def line_gathered(value, axis):
    lower, upper, up, down = [], [], value, value
    for _ in range(lax.axis_size(axis) - 1):
        up, down = shifted(up, axis, 1), shifted(down, axis, -1)
        lower.append(up)
        upper.append(down)
    return lower, upper


def exchanged(parts, axis):
    return [parts[0]] + [rotated(parts[k], axis, k) for k in range(1, len(parts))]


def summed(value, axis):
    n = lax.axis_size(axis)
    if n <= 4:
        return sum((rotated(value, axis, k) for k in range(1, n)), value)
    hop = 1
    while hop < n:
        value, hop = value + swapped(value, axis, hop), 2 * hop
    return value


def local(
    encoded,
    sent_forward,
    head_cotangent,
    grad_sent,
    x_saved,
    q_saved,
    k_saved,
    v_saved,
    norm_gain,
    logit_scale,
    w_query,
    w_key,
    w_value,
    w_out,
    key_blocks,
    key_counts,
):
    n_dp = lax.axis_size("dp")
    factor = logit_scale / math.sqrt(HD)
    blocks, counts = key_blocks[0], key_counts[0]
    wq, wk, wv, wo = w_query[0], w_key[0], w_value[0], w_out[0]
    q, k, v, x = q_saved[0, 0], k_saved[0, 0], v_saved[0, 0], x_saved[0, 0]

    sent = pick(sent_forward[0, 0], encoded[0], grad_sent[0, 0], head_cotangent[0])
    ins = [crossed(sent, j) for j in range(3)]
    column_sets = column_parts(x, ins[0], norm_gain, n_dp)
    moved = exchanged(column_sets, "dp")
    soft, att = saved_attention(blocks, counts, factor, q, k, v, after=column_sets[:1])
    halves, token = half_relayed(ins[1], ins[2], after=[att, *moved[1:]])
    ins = ins + halves
    atts = exchanged([att] * n_dp, "dp")
    cols = stacked(moved, after=[token])
    cols = [cols] + [swapped(cols, "seq", j) for j in (1, 2)]

    grads = backward_attention(factor, ins, soft, wo, att, q, k, v, after=[cols[0], *atts[1:2]])
    lower, upper = line_gathered(grads, "dp")
    dx_near, dx_far = input_grads(grads, wq, wk, wv)
    dx_far = passed(dx_far, after=cols[1:])
    dx_came = swapped(dx_far, "seq", 1)
    cols = cols + [swapped(cols[1], "seq", 2)]
    mix_near, mix_far = forward_terms(
        blocks,
        counts,
        factor,
        ins,
        norm_gain,
        (wq, wk, wv, wo),
        after=[dx_far, *lower[:1], *upper[:1]],
    )
    mix_came = swapped(mix_far, "seq", 1)
    dx_sum = added(dx_near, dx_came, after=[mix_near])
    dx_last = swapped(dx_sum, "seq", 2)
    back_out, gain_part = back(dx_near, dx_came, dx_last, x, ins[0], norm_gain, after=[cols[3], *lower[1:2], *upper[1:2]])
    mix_sum = added(mix_near, mix_came, after=[back_out, *lower[2:3], *upper[2:3]])
    mix_last = swapped(mix_sum, "seq", 2)

    gain_part = gain_added(gain_part, swapped(gain_part, "seq", 1), after=[mix_sum])
    gain_hop = swapped(gain_part, "seq", 2)
    grad_q, grad_k, grad_v = weight_grads(cols, grads, lower, upper, after=[gain_part])
    gain_part = gain_added(gain_part, gain_hop, after=[grad_q, mix_last])
    grad_out = out_weight_grads(cols, atts, after=[gain_part])
    gain_part = summed(gain_part, "dp")
    total = mix_near[0].astype(F32) + mix_came[0].astype(F32) + mix_last.astype(F32)
    forward_out = (ins[0][1].astype(F32) + total).astype(BF16)

    return (
        forward_out[None, None],
        back_out[None, None],
        grad_q[None],
        grad_k[None],
        grad_v[None],
        grad_out[None],
        gain_part,
    )


def solution(mesh):
    in_specs = (
        P("dp", "seq", None),
        P("pipe", "dp", "seq", None),
        P("dp", "seq", None),
        P("pipe", "dp", "seq", None),
        P("pipe", "dp", "seq", None),
        P("pipe", "dp", None, "seq"),
        P("pipe", "dp", None, "seq"),
        P("pipe", "dp", None, "seq"),
        P("pipe", None),
        P("pipe", "seq"),
        P("pipe", None, "seq"),
        P("pipe", None, "seq"),
        P("pipe", None, "seq"),
        P("pipe", "seq", None),
        P("dp", None, None),
        P("dp", None),
    )
    out_specs = (
        P("pipe", "dp", "seq", None),
        P("pipe", "dp", "seq", None),
        P("pipe", "dp", "seq"),
        P("pipe", "dp", "seq"),
        P("pipe", "dp", "seq"),
        P("pipe", "seq", "dp"),
        P("pipe", None),
    )
    return jax.shard_map(local, mesh=mesh, in_specs=in_specs, out_specs=out_specs, check_vma=False)
```

```python
import functools
import math

import jax
import jax.numpy as jnp
from jax import lax
from jax.experimental import pallas as pl
from jax.experimental.pallas import tpu as pltpu
from jax.sharding import PartitionSpec as P

HD = 128
BLOCK = 128
EPSILON = 1e-05
CHUNK = 512
MIB = 1024 * 1024

BF16 = jnp.bfloat16
F32 = jnp.float32
HBM = pl.BlockSpec(memory_space=pl.ANY)
VMEM = pl.BlockSpec(memory_space=pltpu.VMEM)
SMEM = pl.BlockSpec(memory_space=pltpu.SMEM)


def dot_nn(a, b):
    return lax.dot_general(a, b, (((1,), (0,)), ((), ())), preferred_element_type=F32)


def dot_nt(a, b):
    return lax.dot_general(a, b, (((1,), (1,)), ((), ())), preferred_element_type=F32)


def dot_tn(a, b):
    return lax.dot_general(a, b, (((0,), (0,)), ((), ())), preferred_element_type=F32)


def sds(shape, dtype):
    return jax.ShapeDtypeStruct(shape, dtype)


def params(grid=0):
    semantics = ("arbitrary",) * grid if grid else None
    return pltpu.CompilerParams(vmem_limit_bytes=64 * MIB, dimension_semantics=semantics)


SMALL = pl.CostEstimate(flops=1024, bytes_accessed=1024, transcendentals=0)


def run_copies(copies):
    for copy in copies:
        copy.start()
    for copy in copies:
        copy.wait()


def carry(pairs, held, sems):
    loads = [pltpu.make_async_copy(a, held.at[i], sems.at[0, i]) for i, (a, _) in enumerate(pairs)]
    stores = [pltpu.make_async_copy(held.at[i], b, sems.at[1, i]) for i, (_, b) in enumerate(pairs)]
    for load in loads:
        load.start()
    for load, store in zip(loads, stores):
        load.wait()
        store.start()
    for store in stores:
        store.wait()


def carry_scratch(count, rows, width):
    return [pltpu.VMEM((count, rows, width), BF16), pltpu.SemaphoreType.DMA((2, count))]


def row_pieces(source, target):
    return [
        (source.at[pl.ds(at, 16)], target.at[pl.ds(at, 16)]) for at in range(0, source.shape[0], 16)
    ]


def normalized(rows, gain):
    widened = rows.astype(F32)
    inverse = lax.rsqrt(jnp.mean(widened * widened, axis=-1, keepdims=True) + EPSILON)
    unit = widened * inverse
    return unit, inverse, (unit * gain).astype(BF16)


def seen_pairs(blocks_ref, counts_ref, tokens):
    count, slots = blocks_ref.shape
    row_block = lax.broadcasted_iota(jnp.int32, (tokens, tokens), 0) // BLOCK
    col_block = lax.broadcasted_iota(jnp.int32, (tokens, tokens), 1) // BLOCK
    seen = jnp.zeros((tokens, tokens), jnp.int32)
    for i in range(count):
        for j in range(count):
            flag = jnp.int32(0)
            for t in range(slots):
                listed = (t < counts_ref[i]) & (blocks_ref[i, t] == j)
                flag = flag | listed.astype(jnp.int32)
            seen = jnp.where((row_block == i) & (col_block == j), flag, seen)
    return seen


def soft_scores(query, key, factor, seen):
    scores = dot_nt(query, key) * factor
    scores = jnp.where(seen > 0, scores, -1e30)
    lifted = jnp.exp(scores - jnp.max(scores, axis=-1, keepdims=True))
    return lifted / jnp.sum(lifted, axis=-1, keepdims=True)


def pick_kernel(forward_ref, encoded_ref, grad_ref, head_ref, out_ref, held, sems):
    section = lax.axis_index("pipe")

    def both(first, second):
        carry(row_pieces(first, out_ref.at[0]) + row_pieces(second, out_ref.at[1]), held, sems)

    @pl.when(section == 0)
    def _():
        both(head_ref, forward_ref)

    @pl.when(section != 0)
    def _():
        both(grad_ref, encoded_ref)


def pick(sent_forward, encoded, grad_sent, head):
    rows, model = encoded.shape
    return pl.pallas_call(
        pick_kernel,
        out_shape=sds((2, rows, model), BF16),
        in_specs=[HBM] * 4,
        out_specs=HBM,
        scratch_shapes=carry_scratch(rows // 8, 16, model),
        compiler_params=params(),
        cost_estimate=SMALL,
        name="pick",
    )(sent_forward, encoded, grad_sent, head)


def columns_kernel(x_ref, ins_ref, gain_ref, *rest):
    outs, held = rest[:-1], rest[-1]
    me = lax.axis_index("dp")
    n = len(outs)
    width = outs[0].shape[-1]
    held[...] = normalized(x_ref[...], gain_ref[...])[2]
    for k, out in enumerate(outs):
        start = pl.multiple_of(lax.rem(me + k, n) * width, width)
        out[0] = held[:, pl.ds(start, width)]
        out[1] = ins_ref[0, :, pl.ds(start, width)]


def column_parts(x, ins, gain, n):
    rows, width = x.shape
    part = (2, rows, width // n)
    return pl.pallas_call(
        columns_kernel,
        out_shape=tuple(sds(part, BF16) for _ in range(n)),
        scratch_shapes=[pltpu.VMEM((rows, width), BF16)],
        compiler_params=params(),
        cost_estimate=SMALL,
        name="columns",
    )(x, ins, gain)


def saved_kernel(blocks_ref, counts_ref, factor_ref, q_ref, k_ref, v_ref, *rest):
    soft_ref, att_ref = rest[-2:]
    tokens, width = q_ref.shape
    seen = seen_pairs(blocks_ref, counts_ref, tokens)
    for h in range(width // HD):
        cols = slice(h * HD, (h + 1) * HD)
        soft = soft_scores(q_ref[:, cols], k_ref[:, cols], factor_ref[0, h], seen)
        soft_ref[h] = soft
        att_ref[:, cols] = dot_nn(soft.astype(BF16), v_ref[:, cols]).astype(BF16)


def saved_attention(blocks, counts, factor, q, k, v, after=()):
    tokens, width = q.shape
    heads = width // HD
    return pl.pallas_call(
        saved_kernel,
        out_shape=(sds((heads, tokens, tokens), F32), sds((tokens, width), BF16)),
        in_specs=[SMEM] * 3 + [VMEM] * 3 + [HBM] * len(after),
        compiler_params=params(),
        cost_estimate=SMALL,
        name="saved_attention",
    )(blocks, counts, factor, q, k, v, *after)


def placed(refs, which):
    return [ref.at[which] for ref in refs[:3]] + [refs[3]]


def block_copies(refs, which, held, sems):
    me = lax.axis_index("seq")
    rows = refs[0].shape[1]
    copies = []
    for j, ref in enumerate(refs):
        at = (me ^ min(j, 3)) * rows + (rows // 2 if j == 4 else 0)
        spot = held.at[pl.ds(pl.multiple_of(at, rows // 2), ref.shape[1])]
        copies.append(pltpu.make_async_copy(ref.at[which], spot, sems.at[j]))
    return copies


def split_rows(held, near_ref, far_ref, first, second, cols_in, cols_out):
    me = lax.axis_index("seq")
    rows = near_ref.shape[1]
    for ref, hop in ((near_ref, 0), (far_ref, first)):
        for i, other in enumerate((0, second)):
            at = pl.multiple_of((me ^ hop ^ other) * rows, rows)
            ref[i, :, cols_out] = held[pl.ds(at, rows), cols_in]


LOADS = 8


def chunk_loads(source, held, sems):
    rows = source.shape[0] // LOADS
    return [
        pltpu.make_async_copy(
            source.at[pl.ds(i * rows, rows)], held.at[pl.ds(i * rows, rows)], sems.at[i]
        )
        for i in range(LOADS)
    ]


def start_all(copies):
    for copy in copies:
        copy.start()


def wait_all(copies):
    for copy in copies:
        copy.wait()


def backward_kernel(n, factor_ref, *rest):
    cots, rest = rest[:n], rest[n:]
    soft_in, source, att_ref, q_ref, k_ref, v_ref = rest[:6]
    out_ref, held, soft_ref, low, wo, sems, soft_sem, w_sems = rest[-8:]
    width = q_ref.shape[1]
    copies = block_copies(cots, 0, held, sems)
    loads = chunk_loads(source, wo, w_sems)
    load_soft = pltpu.make_async_copy(soft_in, soft_ref, soft_sem.at[0])
    start_all(copies)
    start_all(loads)
    wait_all(copies)
    load_soft.start()
    wait_all(loads)
    low[...] = dot_nt(held[...], wo[...]).astype(BF16)
    load_soft.wait()
    for h in range(width // HD):
        cols = slice(h * HD, (h + 1) * HD)
        cot = low[:, cols]
        soft = soft_ref[h]
        products = cot.astype(F32) * att_ref[:, cols].astype(F32)
        dots = jnp.sum(products, axis=-1, keepdims=True)
        grads = soft * (dot_nt(cot, v_ref[:, cols]) - dots) * factor_ref[0, h]
        grads = grads.astype(BF16)
        soft = soft.astype(BF16)
        out_ref[:, h * HD : (h + 1) * HD] = dot_nn(grads, k_ref[:, cols]).astype(BF16)
        key_at = width + h * HD
        out_ref[:, key_at : key_at + HD] = dot_tn(grads, q_ref[:, cols]).astype(BF16)
        value_at = 2 * width + h * HD
        out_ref[:, value_at : value_at + HD] = dot_tn(soft, cot).astype(BF16)


def backward_attention(factor, cots, soft, wo, att, q, k, v, after=()):
    tokens, width = q.shape
    n = len(cots)
    return pl.pallas_call(
        functools.partial(backward_kernel, n),
        out_shape=sds((tokens, 3 * width), BF16),
        in_specs=[SMEM] + [HBM] * (n + 2) + [VMEM] * 4 + [HBM] * len(after),
        scratch_shapes=[
            pltpu.VMEM((tokens, wo.shape[1]), BF16),
            pltpu.VMEM(soft.shape, F32),
            pltpu.VMEM((tokens, width), BF16),
            pltpu.VMEM(wo.shape, BF16),
            pltpu.SemaphoreType.DMA((n,)),
            pltpu.SemaphoreType.DMA((1,)),
            pltpu.SemaphoreType.DMA((LOADS,)),
        ],
        compiler_params=params(),
        cost_estimate=SMALL,
        name="backward_attention",
    )(factor, *cots, soft, wo, att, q, k, v, *after)


def input_grad_kernel(g_ref, *rest):
    near_ref, far_ref, tile, wq, wk, wv, sems = rest[-7:]
    rows, width = wq.shape[0] // LOADS, wq.shape[1]
    groups = list(
        zip(*(chunk_loads(rest[i], w, sems.at[i]) for i, w in enumerate((wq, wk, wv))))
    )
    for group in groups[:3]:
        start_all(group)
    for i, group in enumerate(groups):
        wait_all(group)
        if i + 3 < LOADS:
            start_all(groups[i + 3])
        at = slice(i * rows, (i + 1) * rows)
        total = dot_nt(g_ref[:, :width], wq[at, :])
        total += dot_nt(g_ref[:, width : 2 * width], wk[at, :])
        total += dot_nt(g_ref[:, 2 * width :], wv[at, :])
        tile[...] = total.astype(BF16)
        split_rows(tile, near_ref, far_ref, 1, 2, slice(None), at)


def input_grads(grads, wq, wk, wv, after=()):
    tokens = grads.shape[0]
    model = wq.shape[0]
    return pl.pallas_call(
        input_grad_kernel,
        out_shape=(sds((2, tokens // 4, model), BF16),) * 2,
        in_specs=[VMEM] + [HBM] * (3 + len(after)),
        scratch_shapes=[pltpu.VMEM((tokens, model // LOADS), BF16)]
        + [pltpu.VMEM(wq.shape, BF16)] * 3
        + [pltpu.SemaphoreType.DMA((3, LOADS))],
        compiler_params=params(),
        cost_estimate=SMALL,
        name="input_grads",
    )(grads, wq, wk, wv, *after)


def forward_kernel(n, blocks_ref, counts_ref, factor_ref, *rest):
    xs, rest = rest[:n], rest[n:]
    gain_ref, sources = rest[0], rest[1:5]
    near_ref, far_ref, held, low, att, wq, wk, wv, wo, sems, w_sems = rest[-11:]
    copies = block_copies(xs, 1, held, sems)
    loads = [
        chunk_loads(source, w, w_sems.at[i])
        for i, (source, w) in enumerate(zip(sources, (wq, wk, wv, wo)))
    ]
    start_all(copies)
    start_all(loads[0])
    wait_all(copies)
    tokens = held.shape[0]
    width = wq.shape[1]

    @pl.loop(0, tokens // 32)
    def _(i):
        at = pl.ds(pl.multiple_of(i * 32, 32), 32)
        held[at, :] = normalized(held[at, :], gain_ref[...])[2]

    for i, w in enumerate((wq, wk, wv)):
        start_all(loads[i + 1])
        wait_all(loads[i])
        low[:, i * width : (i + 1) * width] = dot_nn(held[...], w[...]).astype(BF16)
    seen = seen_pairs(blocks_ref, counts_ref, tokens)
    for h in range(width // HD):
        query, key, value = (
            low[:, i * width + h * HD : i * width + (h + 1) * HD] for i in range(3)
        )
        soft = soft_scores(query, key, factor_ref[0, h], seen)
        att[:, h * HD : (h + 1) * HD] = dot_nn(soft.astype(BF16), value).astype(BF16)
    wait_all(loads[3])
    for i in range(wo.shape[1] // CHUNK):
        at = slice(i * CHUNK, (i + 1) * CHUNK)
        held[:, at] = dot_nn(att[...], wo[:, at]).astype(BF16)
        split_rows(held, near_ref, far_ref, 1, 2, at, at)


def forward_terms(blocks, counts, factor, xs, gain, weights, after=()):
    n = len(xs)
    _, rows, model = xs[0].shape
    width = weights[0].shape[1]
    tokens = 4 * rows
    return pl.pallas_call(
        functools.partial(forward_kernel, n),
        out_shape=(sds((2, rows, model), BF16),) * 2,
        in_specs=[SMEM] * 3 + [HBM] * n + [VMEM] + [HBM] * (4 + len(after)),
        scratch_shapes=[
            pltpu.VMEM((tokens, model), BF16),
            pltpu.VMEM((tokens, 3 * width), BF16),
            pltpu.VMEM((tokens, width), BF16),
        ]
        + [pltpu.VMEM(w.shape, BF16) for w in weights]
        + [pltpu.SemaphoreType.DMA((n,)), pltpu.SemaphoreType.DMA((4, LOADS))],
        compiler_params=params(),
        cost_estimate=SMALL,
        name="forward_terms",
    )(blocks, counts, factor, *xs, gain, *weights, *after)


def back_kernel(near_ref, came_ref, last_ref, x_ref, ins_ref, gain_ref, *rest):
    back_ref, part_ref = rest[-2:]
    gain = gain_ref[...]
    unit, inverse, _ = normalized(x_ref[...], gain)
    grad = near_ref[0].astype(F32) + came_ref[0].astype(F32) + last_ref[...].astype(F32)
    scaled = gain * grad
    part_ref[...] = jnp.sum(grad * unit, axis=0, keepdims=True)
    inner = jnp.mean(scaled * unit, axis=-1, keepdims=True)
    back_ref[...] = (ins_ref[0].astype(F32) + inverse * (scaled - unit * inner)).astype(BF16)


def back(near, came, last, x, ins, gain, after=()):
    return pl.pallas_call(
        back_kernel,
        out_shape=(sds(x.shape, BF16), sds(gain.shape, F32)),
        in_specs=[VMEM] * 6 + [HBM] * len(after),
        compiler_params=params(),
        cost_estimate=SMALL,
        name="back",
    )(near, came, last, x, ins, gain, *after)


def ring_device(place, n):
    return 2 * place if place < (n + 1) // 2 else 2 * (n - 1 - place) + 1


def slice_copies(which, parts, cols, sems):
    seq, dp = lax.axis_index("seq"), lax.axis_index("dp")
    copies = []
    for j, part in enumerate(parts):
        _, n, rows, _ = part.shape
        at = pl.ds(pl.multiple_of((seq ^ j) * rows, rows), rows)
        for k in range(n):
            sample = lax.rem(dp + n - k, n)
            source = part.at[which, k]
            copies.append(pltpu.make_async_copy(source, cols.at[sample, at], sems.at[j, k]))
    return copies


def weight_kernel(n_seq, n_dp, *rest):
    parts, factors_in = rest[:n_seq], rest[n_seq : n_seq + n_dp]
    out_q, out_k, out_v, cols, grads, sems, own_sems = rest[-7:]
    me = lax.axis_index("dp")
    half = me // 2
    place = jnp.where(me % 2 == 0, half, n_dp - 1 - half)
    copies = slice_copies(0, parts, cols, sems)
    for t, source in enumerate(factors_in):
        before = lax.rem(place + n_dp - t, n_dp)
        sample = jnp.where(before < (n_dp + 1) // 2, 2 * before, 2 * (n_dp - 1 - before) + 1)
        copies.append(pltpu.make_async_copy(source, grads.at[sample], own_sems.at[t]))
    run_copies(copies)
    width = out_q.shape[1]
    tile = min(512, out_q.shape[0])
    samples, tokens, _ = cols.shape

    @pl.loop(0, out_q.shape[0] // tile)
    def _(i):
        at = pl.ds(pl.multiple_of(i * tile, tile), tile)
        total = dot_tn(
            cols[:, :, at].reshape(samples * tokens, tile),
            grads[...].reshape(samples * tokens, 3 * width),
        ).astype(BF16)
        for o, out in enumerate((out_q, out_k, out_v)):
            out[at, :] = total[:, o * width : (o + 1) * width]


def out_weight_kernel(n_seq, n_dp, *rest):
    parts, factors_in = rest[:n_seq], rest[n_seq : n_seq + n_dp]
    out_ref, cols, factors, sems, own_sems = rest[-5:]
    dp = lax.axis_index("dp")
    copies = slice_copies(1, parts, cols, sems)
    for k, source in enumerate(factors_in):
        spot = factors.at[lax.rem(dp + n_dp - k, n_dp)]
        copies.append(pltpu.make_async_copy(source, spot, own_sems.at[k]))
    run_copies(copies)
    samples, tokens, slice_width = cols.shape
    tile = 512

    @pl.loop(0, out_ref.shape[0] // tile)
    def _(i):
        at = pl.ds(pl.multiple_of(i * tile, tile), tile)
        out_ref[at, :] = dot_tn(
            factors[:, :, at].reshape(samples * tokens, tile),
            cols[...].reshape(samples * tokens, slice_width),
        ).astype(BF16)


def contracted(kernel, name, parts, factors, out_shape, after=()):
    _, samples, rows, slice_width = parts[0].shape
    tokens, width = factors[0].shape
    return pl.pallas_call(
        functools.partial(kernel, len(parts), samples),
        out_shape=out_shape,
        in_specs=[HBM] * (len(parts) + len(factors) + len(after)),
        scratch_shapes=[
            pltpu.VMEM((samples, len(parts) * rows, slice_width), BF16),
            pltpu.VMEM((samples, tokens, width), BF16),
            pltpu.SemaphoreType.DMA((len(parts), samples)),
            pltpu.SemaphoreType.DMA((samples,)),
        ],
        compiler_params=params(),
        cost_estimate=SMALL,
        name=name,
    )(*parts, *factors, *after)


def weight_grads(parts, grads, after=()):
    shape = sds((parts[0].shape[3], grads[0].shape[1] // 3), BF16)
    return contracted(weight_kernel, "weight_grads", parts, grads, (shape,) * 3, after)


def out_weight_grads(parts, atts, after=()):
    shape = sds((atts[0].shape[1], parts[0].shape[3]), BF16)
    return contracted(out_weight_kernel, "out_weight_grads", parts, atts, shape, after)


def half_relay_kernel(first_ref, second_ref, *rest):
    for_x, for_y, held, sems = rest[-4:]
    pair, half, _ = for_x.shape
    pairs = []
    for i in range(pair):
        pairs += row_pieces(second_ref.at[i, pl.ds(0, half)], for_x.at[i])
        pairs += row_pieces(first_ref.at[i, pl.ds(half, half)], for_y.at[i])
    carry(pairs, held, sems)


def half_relayed(first, second, after=()):
    pair, rows, model = first.shape
    for_x, for_y = pl.pallas_call(
        half_relay_kernel,
        out_shape=(sds((pair, rows // 2, model), BF16),) * 2,
        in_specs=[HBM] * (2 + len(after)),
        out_specs=(HBM, HBM),
        scratch_shapes=carry_scratch(pair * rows // 16, 16, model),
        compiler_params=params(),
        cost_estimate=SMALL,
        name="half_relay",
    )(first, second, *after)
    return [swapped(for_x, "seq", 1), swapped(for_y, "seq", 2)], for_x


def stack_kernel(n, *rest):
    out_ref, held, sems = rest[-3:]
    carry([(rest[k].at[i], out_ref.at[i, k]) for i in range(2) for k in range(n)], held, sems)


def stacked(parts, after=()):
    n = len(parts)
    pair, rows, width = parts[0].shape
    return pl.pallas_call(
        functools.partial(stack_kernel, n),
        out_shape=sds((pair, n, rows, width), BF16),
        in_specs=[HBM] * (n + len(after)),
        out_specs=HBM,
        scratch_shapes=carry_scratch(pair * n, rows, width),
        compiler_params=params(),
        cost_estimate=SMALL,
        name="stack",
    )(*parts, *after)


def add_kernel(near_ref, came_ref, *rest):
    out_ref, near, came, sems = rest[-4:]
    run_copies(
        [
            pltpu.make_async_copy(near_ref.at[1], near, sems.at[0]),
            pltpu.make_async_copy(came_ref.at[1], came, sems.at[1]),
        ]
    )
    out_ref[...] = (near[...].astype(F32) + came[...].astype(F32)).astype(BF16)


def added(near, came, after=()):
    shape = near.shape[1:]
    return pl.pallas_call(
        add_kernel,
        out_shape=sds(shape, BF16),
        in_specs=[HBM] * (2 + len(after)),
        scratch_shapes=[
            pltpu.VMEM(shape, BF16),
            pltpu.VMEM(shape, BF16),
            pltpu.SemaphoreType.DMA((2,)),
        ],
        compiler_params=params(),
        cost_estimate=SMALL,
        name="add",
    )(near, came, *after)


def passed_kernel(value_ref, *rest):
    out_ref, held, sems = rest[-3:]
    carry(row_pieces(value_ref.at[0], out_ref.at[0]) + row_pieces(value_ref.at[1], out_ref.at[1]), held, sems)


def passed(value, after):
    pair, rows, model = value.shape
    return pl.pallas_call(
        passed_kernel,
        out_shape=sds(value.shape, value.dtype),
        in_specs=[HBM] * (1 + len(after)),
        out_specs=HBM,
        scratch_shapes=carry_scratch(pair * rows // 16, 16, model),
        compiler_params=params(),
        cost_estimate=SMALL,
        name="passed",
    )(value, *after)


def gain_kernel(own_ref, came_ref, *rest):
    rest[-1][...] = own_ref[...] + came_ref[...]


def gain_added(own, came, after=()):
    return pl.pallas_call(
        gain_kernel,
        out_shape=sds(own.shape, F32),
        in_specs=[VMEM] * 2 + [HBM] * len(after),
        compiler_params=params(),
        cost_estimate=SMALL,
        name="gain_added",
    )(own, came, *after)


def swapped(value, axis, j):
    return lax.ppermute(value, axis, [(i, i ^ j) for i in range(lax.axis_size(axis))])


def crossed(value, j):
    n = lax.axis_size("seq")
    pairs = [(p * n + i, (1 - p) * n + (i ^ j)) for p in range(2) for i in range(n)]
    return lax.ppermute(value, ("pipe", "seq"), pairs)


def rotated(value, axis, k):
    n = lax.axis_size(axis)
    return lax.ppermute(value, axis, [(i, (i + k) % n) for i in range(n)])


def ring_gathered(value, axis):
    n = lax.axis_size(axis)
    pairs = [(ring_device(p, n), ring_device((p + 1) % n, n)) for p in range(n)]
    values = [value]
    for _ in range(n - 1):
        values.append(lax.ppermute(values[-1], axis, pairs))
    return values


def exchanged(parts, axis):
    return [parts[0]] + [rotated(parts[k], axis, k) for k in range(1, len(parts))]


def summed(value, axis):
    n = lax.axis_size(axis)
    if n <= 4:
        return sum((rotated(value, axis, k) for k in range(1, n)), value)
    hop = 1
    while hop < n:
        value, hop = value + swapped(value, axis, hop), 2 * hop
    return value


def local(
    encoded,
    sent_forward,
    head_cotangent,
    grad_sent,
    x_saved,
    q_saved,
    k_saved,
    v_saved,
    norm_gain,
    logit_scale,
    w_query,
    w_key,
    w_value,
    w_out,
    key_blocks,
    key_counts,
):
    n_dp = lax.axis_size("dp")
    factor = logit_scale / math.sqrt(HD)
    blocks, counts = key_blocks[0], key_counts[0]
    wq, wk, wv, wo = w_query[0], w_key[0], w_value[0], w_out[0]
    q, k, v, x = q_saved[0, 0], k_saved[0, 0], v_saved[0, 0], x_saved[0, 0]

    sent = pick(sent_forward[0, 0], encoded[0], grad_sent[0, 0], head_cotangent[0])
    ins = [crossed(sent, j) for j in range(3)]
    column_sets = column_parts(x, ins[0], norm_gain, n_dp)
    moved = exchanged(column_sets, "dp")
    soft, att = saved_attention(blocks, counts, factor, q, k, v, after=column_sets[:1])
    halves, token = half_relayed(ins[1], ins[2], after=[att, *moved[1:]])
    ins = ins + halves
    atts = exchanged([att] * n_dp, "dp")
    cols = stacked(moved, after=[token])
    cols = [cols] + [swapped(cols, "seq", j) for j in (1, 2)]

    grads = backward_attention(factor, ins, soft, wo, att, q, k, v, after=[cols[0], *atts[1:2]])
    ring = ring_gathered(grads, "dp")
    dx_near, dx_far = input_grads(grads, wq, wk, wv)
    dx_far = passed(dx_far, after=cols[1:])
    dx_came = swapped(dx_far, "seq", 1)
    cols = cols + [swapped(cols[1], "seq", 2)]
    mix_near, mix_far = forward_terms(
        blocks,
        counts,
        factor,
        ins,
        norm_gain,
        (wq, wk, wv, wo),
        after=[dx_far, *ring[1:2]],
    )
    mix_came = swapped(mix_far, "seq", 1)
    dx_sum = added(dx_near, dx_came, after=[mix_near])
    dx_last = swapped(dx_sum, "seq", 2)
    back_out, gain_part = back(dx_near, dx_came, dx_last, x, ins[0], norm_gain, after=[cols[3], *ring[2:3], *atts[3:]])
    mix_sum = added(mix_near, mix_came, after=[back_out, *ring[3:4]])
    mix_last = swapped(mix_sum, "seq", 2)

    gain_part = gain_added(gain_part, swapped(gain_part, "seq", 1), after=[mix_sum])
    gain_hop = swapped(gain_part, "seq", 2)
    grad_q, grad_k, grad_v = weight_grads(cols, ring, after=[gain_part])
    gain_part = gain_added(gain_part, gain_hop, after=[grad_q, mix_last])
    grad_out = out_weight_grads(cols, atts, after=[gain_part])
    gain_part = summed(gain_part, "dp")
    total = mix_near[0].astype(F32) + mix_came[0].astype(F32) + mix_last.astype(F32)
    forward_out = (ins[0][1].astype(F32) + total).astype(BF16)

    return (
        forward_out[None, None],
        back_out[None, None],
        grad_q[None],
        grad_k[None],
        grad_v[None],
        grad_out[None],
        gain_part,
    )


def solution(mesh):
    in_specs = (
        P("dp", "seq", None),
        P("pipe", "dp", "seq", None),
        P("dp", "seq", None),
        P("pipe", "dp", "seq", None),
        P("pipe", "dp", "seq", None),
        P("pipe", "dp", None, "seq"),
        P("pipe", "dp", None, "seq"),
        P("pipe", "dp", None, "seq"),
        P("pipe", None),
        P("pipe", "seq"),
        P("pipe", None, "seq"),
        P("pipe", None, "seq"),
        P("pipe", None, "seq"),
        P("pipe", "seq", None),
        P("dp", None, None),
        P("dp", None),
    )
    out_specs = (
        P("pipe", "dp", "seq", None),
        P("pipe", "dp", "seq", None),
        P("pipe", "dp", "seq"),
        P("pipe", "dp", "seq"),
        P("pipe", "dp", "seq"),
        P("pipe", "seq", "dp"),
        P("pipe", None),
    )
    return jax.shard_map(local, mesh=mesh, in_specs=in_specs, out_specs=out_specs, check_vma=False)
```

```python
import functools
import math

import jax
import jax.numpy as jnp
from jax import lax
from jax.experimental import pallas as pl
from jax.experimental.pallas import tpu as pltpu
from jax.sharding import PartitionSpec as P

HD = 128
BLOCK = 128
EPSILON = 1e-05
CHUNK = 512
MIB = 1024 * 1024

BF16 = jnp.bfloat16
F32 = jnp.float32
HBM = pl.BlockSpec(memory_space=pl.ANY)
VMEM = pl.BlockSpec(memory_space=pltpu.VMEM)
SMEM = pl.BlockSpec(memory_space=pltpu.SMEM)


def dot_nn(a, b):
    return lax.dot_general(a, b, (((1,), (0,)), ((), ())), preferred_element_type=F32)


def dot_nt(a, b):
    return lax.dot_general(a, b, (((1,), (1,)), ((), ())), preferred_element_type=F32)


def dot_tn(a, b):
    return lax.dot_general(a, b, (((0,), (0,)), ((), ())), preferred_element_type=F32)


def sds(shape, dtype):
    return jax.ShapeDtypeStruct(shape, dtype)


def params(grid=0):
    semantics = ("arbitrary",) * grid if grid else None
    return pltpu.CompilerParams(vmem_limit_bytes=64 * MIB, dimension_semantics=semantics)


SMALL = pl.CostEstimate(flops=1024, bytes_accessed=1024, transcendentals=0)


def run_copies(copies):
    for copy in copies:
        copy.start()
    for copy in copies:
        copy.wait()


def carry(pairs, held, sems):
    loads = [pltpu.make_async_copy(a, held.at[i], sems.at[0, i]) for i, (a, _) in enumerate(pairs)]
    stores = [pltpu.make_async_copy(held.at[i], b, sems.at[1, i]) for i, (_, b) in enumerate(pairs)]
    for load in loads:
        load.start()
    for load, store in zip(loads, stores):
        load.wait()
        store.start()
    for store in stores:
        store.wait()


def carry_scratch(count, rows, width):
    return [pltpu.VMEM((count, rows, width), BF16), pltpu.SemaphoreType.DMA((2, count))]


def row_pieces(source, target):
    return [
        (source.at[pl.ds(at, 16)], target.at[pl.ds(at, 16)]) for at in range(0, source.shape[0], 16)
    ]


def normalized(rows, gain):
    widened = rows.astype(F32)
    inverse = lax.rsqrt(jnp.mean(widened * widened, axis=-1, keepdims=True) + EPSILON)
    unit = widened * inverse
    return unit, inverse, (unit * gain).astype(BF16)


def seen_pairs(blocks_ref, counts_ref, tokens):
    count, slots = blocks_ref.shape
    row_block = lax.broadcasted_iota(jnp.int32, (tokens, tokens), 0) // BLOCK
    col_block = lax.broadcasted_iota(jnp.int32, (tokens, tokens), 1) // BLOCK
    seen = jnp.zeros((tokens, tokens), jnp.int32)
    for i in range(count):
        for j in range(count):
            flag = jnp.int32(0)
            for t in range(slots):
                listed = (t < counts_ref[i]) & (blocks_ref[i, t] == j)
                flag = flag | listed.astype(jnp.int32)
            seen = jnp.where((row_block == i) & (col_block == j), flag, seen)
    return seen


def soft_scores(query, key, factor, seen):
    scores = dot_nt(query, key) * factor
    scores = jnp.where(seen > 0, scores, -1e30)
    lifted = jnp.exp(scores - jnp.max(scores, axis=-1, keepdims=True))
    return lifted / jnp.sum(lifted, axis=-1, keepdims=True)


def pick_kernel(forward_ref, encoded_ref, grad_ref, head_ref, out_ref, held, sems):
    section = lax.axis_index("pipe")

    def both(first, second):
        carry(row_pieces(first, out_ref.at[0]) + row_pieces(second, out_ref.at[1]), held, sems)

    @pl.when(section == 0)
    def _():
        both(head_ref, forward_ref)

    @pl.when(section != 0)
    def _():
        both(grad_ref, encoded_ref)


def pick(sent_forward, encoded, grad_sent, head):
    rows, model = encoded.shape
    return pl.pallas_call(
        pick_kernel,
        out_shape=sds((2, rows, model), BF16),
        in_specs=[HBM] * 4,
        out_specs=HBM,
        scratch_shapes=carry_scratch(rows // 8, 16, model),
        compiler_params=params(),
        cost_estimate=SMALL,
        name="pick",
    )(sent_forward, encoded, grad_sent, head)


def columns_kernel(x_ref, ins_ref, gain_ref, *rest):
    outs, held = rest[:-1], rest[-1]
    me = lax.axis_index("dp")
    n = len(outs)
    width = outs[0].shape[-1]
    held[...] = normalized(x_ref[...], gain_ref[...])[2]
    for k, out in enumerate(outs):
        start = pl.multiple_of(lax.rem(me + k, n) * width, width)
        out[0] = held[:, pl.ds(start, width)]
        out[1] = ins_ref[0, :, pl.ds(start, width)]


def column_parts(x, ins, gain, n):
    rows, width = x.shape
    part = (2, rows, width // n)
    return pl.pallas_call(
        columns_kernel,
        out_shape=tuple(sds(part, BF16) for _ in range(n)),
        scratch_shapes=[pltpu.VMEM((rows, width), BF16)],
        compiler_params=params(),
        cost_estimate=SMALL,
        name="columns",
    )(x, ins, gain)


def saved_kernel(blocks_ref, counts_ref, factor_ref, q_ref, k_ref, v_ref, *rest):
    soft_ref, att_ref = rest[-2:]
    tokens, width = q_ref.shape
    seen = seen_pairs(blocks_ref, counts_ref, tokens)
    for h in range(width // HD):
        cols = slice(h * HD, (h + 1) * HD)
        soft = soft_scores(q_ref[:, cols], k_ref[:, cols], factor_ref[0, h], seen)
        soft_ref[h] = soft
        att_ref[:, cols] = dot_nn(soft.astype(BF16), v_ref[:, cols]).astype(BF16)


def saved_attention(blocks, counts, factor, q, k, v, after=()):
    tokens, width = q.shape
    heads = width // HD
    return pl.pallas_call(
        saved_kernel,
        out_shape=(sds((heads, tokens, tokens), F32), sds((tokens, width), BF16)),
        in_specs=[SMEM] * 3 + [VMEM] * 3 + [HBM] * len(after),
        compiler_params=params(),
        cost_estimate=SMALL,
        name="saved_attention",
    )(blocks, counts, factor, q, k, v, *after)


def placed(refs, which):
    return [ref.at[which] for ref in refs[:3]] + [refs[3]]


def block_copies(refs, which, held, sems):
    me = lax.axis_index("seq")
    rows = refs[0].shape[1]
    copies = []
    for j, ref in enumerate(refs):
        at = (me ^ min(j, 3)) * rows + (rows // 2 if j == 4 else 0)
        spot = held.at[pl.ds(pl.multiple_of(at, rows // 2), ref.shape[1])]
        copies.append(pltpu.make_async_copy(ref.at[which], spot, sems.at[j]))
    return copies


def split_rows(held, near_ref, far_ref, first, second, cols_in, cols_out):
    me = lax.axis_index("seq")
    rows = near_ref.shape[1]
    for ref, hop in ((near_ref, 0), (far_ref, first)):
        for i, other in enumerate((0, second)):
            at = pl.multiple_of((me ^ hop ^ other) * rows, rows)
            ref[i, :, cols_out] = held[pl.ds(at, rows), cols_in]


LOADS = 8


def chunk_loads(source, held, sems):
    rows = source.shape[0] // LOADS
    return [
        pltpu.make_async_copy(
            source.at[pl.ds(i * rows, rows)], held.at[pl.ds(i * rows, rows)], sems.at[i]
        )
        for i in range(LOADS)
    ]


def start_all(copies):
    for copy in copies:
        copy.start()


def wait_all(copies):
    for copy in copies:
        copy.wait()


def backward_kernel(n, factor_ref, *rest):
    cots, rest = rest[:n], rest[n:]
    soft_in, source, att_ref, q_ref, k_ref, v_ref = rest[:6]
    out_ref, held, soft_ref, low, wo, sems, soft_sem, w_sems = rest[-8:]
    width = q_ref.shape[1]
    copies = block_copies(cots, 0, held, sems)
    loads = chunk_loads(source, wo, w_sems)
    load_soft = pltpu.make_async_copy(soft_in, soft_ref, soft_sem.at[0])
    start_all(copies)
    start_all(loads)
    wait_all(copies)
    load_soft.start()
    wait_all(loads)
    low[...] = dot_nt(held[...], wo[...]).astype(BF16)
    load_soft.wait()
    for h in range(width // HD):
        cols = slice(h * HD, (h + 1) * HD)
        cot = low[:, cols]
        soft = soft_ref[h]
        products = cot.astype(F32) * att_ref[:, cols].astype(F32)
        dots = jnp.sum(products, axis=-1, keepdims=True)
        grads = soft * (dot_nt(cot, v_ref[:, cols]) - dots) * factor_ref[0, h]
        grads = grads.astype(BF16)
        soft = soft.astype(BF16)
        out_ref[:, h * HD : (h + 1) * HD] = dot_nn(grads, k_ref[:, cols]).astype(BF16)
        key_at = width + h * HD
        out_ref[:, key_at : key_at + HD] = dot_tn(grads, q_ref[:, cols]).astype(BF16)
        value_at = 2 * width + h * HD
        out_ref[:, value_at : value_at + HD] = dot_tn(soft, cot).astype(BF16)


def backward_attention(factor, cots, soft, wo, att, q, k, v, after=()):
    tokens, width = q.shape
    n = len(cots)
    return pl.pallas_call(
        functools.partial(backward_kernel, n),
        out_shape=sds((tokens, 3 * width), BF16),
        in_specs=[SMEM] + [HBM] * (n + 2) + [VMEM] * 4 + [HBM] * len(after),
        scratch_shapes=[
            pltpu.VMEM((tokens, wo.shape[1]), BF16),
            pltpu.VMEM(soft.shape, F32),
            pltpu.VMEM((tokens, width), BF16),
            pltpu.VMEM(wo.shape, BF16),
            pltpu.SemaphoreType.DMA((n,)),
            pltpu.SemaphoreType.DMA((1,)),
            pltpu.SemaphoreType.DMA((LOADS,)),
        ],
        compiler_params=params(),
        cost_estimate=SMALL,
        name="backward_attention",
    )(factor, *cots, soft, wo, att, q, k, v, *after)


def input_grad_kernel(g_ref, *rest):
    near_ref, far_ref, tile, wq, wk, wv, sems = rest[-7:]
    rows, width = wq.shape[0] // LOADS, wq.shape[1]
    groups = list(
        zip(*(chunk_loads(rest[i], w, sems.at[i]) for i, w in enumerate((wq, wk, wv))))
    )
    for group in groups[:3]:
        start_all(group)
    for i, group in enumerate(groups):
        wait_all(group)
        if i + 3 < LOADS:
            start_all(groups[i + 3])
        at = slice(i * rows, (i + 1) * rows)
        total = dot_nt(g_ref[:, :width], wq[at, :])
        total += dot_nt(g_ref[:, width : 2 * width], wk[at, :])
        total += dot_nt(g_ref[:, 2 * width :], wv[at, :])
        tile[...] = total.astype(BF16)
        split_rows(tile, near_ref, far_ref, 1, 2, slice(None), at)


def input_grads(grads, wq, wk, wv, after=()):
    tokens = grads.shape[0]
    model = wq.shape[0]
    return pl.pallas_call(
        input_grad_kernel,
        out_shape=(sds((2, tokens // 4, model), BF16),) * 2,
        in_specs=[VMEM] + [HBM] * (3 + len(after)),
        scratch_shapes=[pltpu.VMEM((tokens, model // LOADS), BF16)]
        + [pltpu.VMEM(wq.shape, BF16)] * 3
        + [pltpu.SemaphoreType.DMA((3, LOADS))],
        compiler_params=params(),
        cost_estimate=SMALL,
        name="input_grads",
    )(grads, wq, wk, wv, *after)


def forward_kernel(n, blocks_ref, counts_ref, factor_ref, *rest):
    xs, rest = rest[:n], rest[n:]
    gain_ref, sources = rest[0], rest[1:5]
    near_ref, far_ref, held, low, att, wq, wk, wv, wo, sems, w_sems = rest[-11:]
    copies = block_copies(xs, 1, held, sems)
    loads = [
        chunk_loads(source, w, w_sems.at[i])
        for i, (source, w) in enumerate(zip(sources, (wq, wk, wv, wo)))
    ]
    start_all(copies)
    start_all(loads[0])
    wait_all(copies)
    tokens = held.shape[0]
    width = wq.shape[1]

    @pl.loop(0, tokens // 32)
    def _(i):
        at = pl.ds(pl.multiple_of(i * 32, 32), 32)
        held[at, :] = normalized(held[at, :], gain_ref[...])[2]

    for i, w in enumerate((wq, wk, wv)):
        start_all(loads[i + 1])
        wait_all(loads[i])
        low[:, i * width : (i + 1) * width] = dot_nn(held[...], w[...]).astype(BF16)
    seen = seen_pairs(blocks_ref, counts_ref, tokens)
    for h in range(width // HD):
        query, key, value = (
            low[:, i * width + h * HD : i * width + (h + 1) * HD] for i in range(3)
        )
        soft = soft_scores(query, key, factor_ref[0, h], seen)
        att[:, h * HD : (h + 1) * HD] = dot_nn(soft.astype(BF16), value).astype(BF16)
    wait_all(loads[3])
    for i in range(wo.shape[1] // CHUNK):
        at = slice(i * CHUNK, (i + 1) * CHUNK)
        held[:, at] = dot_nn(att[...], wo[:, at]).astype(BF16)
        split_rows(held, near_ref, far_ref, 1, 2, at, at)


def forward_terms(blocks, counts, factor, xs, gain, weights, after=()):
    n = len(xs)
    _, rows, model = xs[0].shape
    width = weights[0].shape[1]
    tokens = 4 * rows
    return pl.pallas_call(
        functools.partial(forward_kernel, n),
        out_shape=(sds((2, rows, model), BF16),) * 2,
        in_specs=[SMEM] * 3 + [HBM] * n + [VMEM] + [HBM] * (4 + len(after)),
        scratch_shapes=[
            pltpu.VMEM((tokens, model), BF16),
            pltpu.VMEM((tokens, 3 * width), BF16),
            pltpu.VMEM((tokens, width), BF16),
        ]
        + [pltpu.VMEM(w.shape, BF16) for w in weights]
        + [pltpu.SemaphoreType.DMA((n,)), pltpu.SemaphoreType.DMA((4, LOADS))],
        compiler_params=params(),
        cost_estimate=SMALL,
        name="forward_terms",
    )(blocks, counts, factor, *xs, gain, *weights, *after)


def back_kernel(near_ref, came_ref, last_ref, x_ref, ins_ref, gain_ref, *rest):
    back_ref, part_ref = rest[-2:]
    gain = gain_ref[...]
    unit, inverse, _ = normalized(x_ref[...], gain)
    grad = near_ref[0].astype(F32) + came_ref[0].astype(F32) + last_ref[...].astype(F32)
    scaled = gain * grad
    part_ref[...] = jnp.sum(grad * unit, axis=0, keepdims=True)
    inner = jnp.mean(scaled * unit, axis=-1, keepdims=True)
    back_ref[...] = (ins_ref[0].astype(F32) + inverse * (scaled - unit * inner)).astype(BF16)


def back(near, came, last, x, ins, gain, after=()):
    return pl.pallas_call(
        back_kernel,
        out_shape=(sds(x.shape, BF16), sds(gain.shape, F32)),
        in_specs=[VMEM] * 6 + [HBM] * len(after),
        compiler_params=params(),
        cost_estimate=SMALL,
        name="back",
    )(near, came, last, x, ins, gain, *after)


def ring_device(place, n):
    return 2 * place if place < (n + 1) // 2 else 2 * (n - 1 - place) + 1


def slice_copies(which, parts, cols, sems):
    seq, dp = lax.axis_index("seq"), lax.axis_index("dp")
    copies = []
    for j, part in enumerate(parts):
        _, n, rows, _ = part.shape
        at = pl.ds(pl.multiple_of((seq ^ j) * rows, rows), rows)
        for k in range(n):
            sample = lax.rem(dp + n - k, n)
            source = part.at[which, k]
            copies.append(pltpu.make_async_copy(source, cols.at[sample, at], sems.at[j, k]))
    return copies


def weight_kernel(n_seq, n_dp, *rest):
    parts, factors_in = rest[:n_seq], rest[n_seq : n_seq + n_dp]
    out_q, out_k, out_v, cols, grads, sems, own_sems = rest[-7:]
    me = lax.axis_index("dp")
    half = me // 2
    place = jnp.where(me % 2 == 0, half, n_dp - 1 - half)
    copies = slice_copies(0, parts, cols, sems)
    for t, source in enumerate(factors_in):
        before = lax.rem(place + n_dp - t, n_dp)
        sample = jnp.where(before < (n_dp + 1) // 2, 2 * before, 2 * (n_dp - 1 - before) + 1)
        copies.append(pltpu.make_async_copy(source, grads.at[sample], own_sems.at[t]))
    run_copies(copies)
    width = out_q.shape[1]
    tile = min(512, out_q.shape[0])
    samples, tokens, _ = cols.shape

    @pl.loop(0, out_q.shape[0] // tile)
    def _(i):
        at = pl.ds(pl.multiple_of(i * tile, tile), tile)
        total = dot_tn(
            cols[:, :, at].reshape(samples * tokens, tile),
            grads[...].reshape(samples * tokens, 3 * width),
        ).astype(BF16)
        for o, out in enumerate((out_q, out_k, out_v)):
            out[at, :] = total[:, o * width : (o + 1) * width]


def out_weight_kernel(n_seq, n_dp, *rest):
    parts, factors_in = rest[:n_seq], rest[n_seq : n_seq + n_dp]
    out_ref, cols, factors, sems, own_sems = rest[-5:]
    dp = lax.axis_index("dp")
    copies = slice_copies(1, parts, cols, sems)
    for k, source in enumerate(factors_in):
        spot = factors.at[lax.rem(dp + n_dp - k, n_dp)]
        copies.append(pltpu.make_async_copy(source, spot, own_sems.at[k]))
    run_copies(copies)
    samples, tokens, slice_width = cols.shape
    tile = 512

    @pl.loop(0, out_ref.shape[0] // tile)
    def _(i):
        at = pl.ds(pl.multiple_of(i * tile, tile), tile)
        out_ref[at, :] = dot_tn(
            factors[:, :, at].reshape(samples * tokens, tile),
            cols[...].reshape(samples * tokens, slice_width),
        ).astype(BF16)


def contracted(kernel, name, parts, factors, out_shape, after=()):
    _, samples, rows, slice_width = parts[0].shape
    tokens, width = factors[0].shape
    return pl.pallas_call(
        functools.partial(kernel, len(parts), samples),
        out_shape=out_shape,
        in_specs=[HBM] * (len(parts) + len(factors) + len(after)),
        scratch_shapes=[
            pltpu.VMEM((samples, len(parts) * rows, slice_width), BF16),
            pltpu.VMEM((samples, tokens, width), BF16),
            pltpu.SemaphoreType.DMA((len(parts), samples)),
            pltpu.SemaphoreType.DMA((samples,)),
        ],
        compiler_params=params(),
        cost_estimate=SMALL,
        name=name,
    )(*parts, *factors, *after)


def weight_grads(parts, grads, after=()):
    shape = sds((parts[0].shape[3], grads[0].shape[1] // 3), BF16)
    return contracted(weight_kernel, "weight_grads", parts, grads, (shape,) * 3, after)


def out_weight_grads(parts, atts, after=()):
    shape = sds((atts[0].shape[1], parts[0].shape[3]), BF16)
    return contracted(out_weight_kernel, "out_weight_grads", parts, atts, shape, after)


def half_relay_kernel(first_ref, second_ref, *rest):
    for_x, for_y, held, sems = rest[-4:]
    pair, half, _ = for_x.shape
    pairs = []
    for i in range(pair):
        pairs += row_pieces(second_ref.at[i, pl.ds(0, half)], for_x.at[i])
        pairs += row_pieces(first_ref.at[i, pl.ds(half, half)], for_y.at[i])
    carry(pairs, held, sems)


def half_relayed(first, second, after=()):
    pair, rows, model = first.shape
    for_x, for_y = pl.pallas_call(
        half_relay_kernel,
        out_shape=(sds((pair, rows // 2, model), BF16),) * 2,
        in_specs=[HBM] * (2 + len(after)),
        out_specs=(HBM, HBM),
        scratch_shapes=carry_scratch(pair * rows // 16, 16, model),
        compiler_params=params(),
        cost_estimate=SMALL,
        name="half_relay",
    )(first, second, *after)
    return [swapped(for_x, "seq", 1), swapped(for_y, "seq", 2)], for_x


def stack_kernel(n, *rest):
    out_ref, held, sems = rest[-3:]
    carry([(rest[k].at[i], out_ref.at[i, k]) for i in range(2) for k in range(n)], held, sems)


def stacked(parts, after=()):
    n = len(parts)
    pair, rows, width = parts[0].shape
    return pl.pallas_call(
        functools.partial(stack_kernel, n),
        out_shape=sds((pair, n, rows, width), BF16),
        in_specs=[HBM] * (n + len(after)),
        out_specs=HBM,
        scratch_shapes=carry_scratch(pair * n, rows, width),
        compiler_params=params(),
        cost_estimate=SMALL,
        name="stack",
    )(*parts, *after)


def add_kernel(near_ref, came_ref, *rest):
    out_ref, near, came, sems = rest[-4:]
    run_copies(
        [
            pltpu.make_async_copy(near_ref.at[1], near, sems.at[0]),
            pltpu.make_async_copy(came_ref.at[1], came, sems.at[1]),
        ]
    )
    out_ref[...] = (near[...].astype(F32) + came[...].astype(F32)).astype(BF16)


def added(near, came, after=()):
    shape = near.shape[1:]
    return pl.pallas_call(
        add_kernel,
        out_shape=sds(shape, BF16),
        in_specs=[HBM] * (2 + len(after)),
        scratch_shapes=[
            pltpu.VMEM(shape, BF16),
            pltpu.VMEM(shape, BF16),
            pltpu.SemaphoreType.DMA((2,)),
        ],
        compiler_params=params(),
        cost_estimate=SMALL,
        name="add",
    )(near, came, *after)


def passed_kernel(value_ref, *rest):
    out_ref, held, sems = rest[-3:]
    carry(row_pieces(value_ref.at[0], out_ref.at[0]) + row_pieces(value_ref.at[1], out_ref.at[1]), held, sems)


def passed(value, after):
    pair, rows, model = value.shape
    return pl.pallas_call(
        passed_kernel,
        out_shape=sds(value.shape, value.dtype),
        in_specs=[HBM] * (1 + len(after)),
        out_specs=HBM,
        scratch_shapes=carry_scratch(pair * rows // 16, 16, model),
        compiler_params=params(),
        cost_estimate=SMALL,
        name="passed",
    )(value, *after)


def gain_kernel(own_ref, came_ref, *rest):
    rest[-1][...] = own_ref[...] + came_ref[...]


def gain_added(own, came, after=()):
    return pl.pallas_call(
        gain_kernel,
        out_shape=sds(own.shape, F32),
        in_specs=[VMEM] * 2 + [HBM] * len(after),
        compiler_params=params(),
        cost_estimate=SMALL,
        name="gain_added",
    )(own, came, *after)


def swapped(value, axis, j):
    return lax.ppermute(value, axis, [(i, i ^ j) for i in range(lax.axis_size(axis))])


def crossed(value, j):
    n = lax.axis_size("seq")
    pairs = [(p * n + i, (1 - p) * n + (i ^ j)) for p in range(2) for i in range(n)]
    return lax.ppermute(value, ("pipe", "seq"), pairs)


def rotated(value, axis, k):
    n = lax.axis_size(axis)
    return lax.ppermute(value, axis, [(i, (i + k) % n) for i in range(n)])


def ring_gathered(value, axis):
    n = lax.axis_size(axis)
    pairs = [(ring_device(p, n), ring_device((p + 1) % n, n)) for p in range(n)]
    values = [value]
    for _ in range(n - 1):
        values.append(lax.ppermute(values[-1], axis, pairs))
    return values


def exchanged(parts, axis):
    return [parts[0]] + [rotated(parts[k], axis, k) for k in range(1, len(parts))]


def summed(value, axis):
    n = lax.axis_size(axis)
    if n <= 4:
        return sum((rotated(value, axis, k) for k in range(1, n)), value)
    hop = 1
    while hop < n:
        value, hop = value + swapped(value, axis, hop), 2 * hop
    return value


def local(
    encoded,
    sent_forward,
    head_cotangent,
    grad_sent,
    x_saved,
    q_saved,
    k_saved,
    v_saved,
    norm_gain,
    logit_scale,
    w_query,
    w_key,
    w_value,
    w_out,
    key_blocks,
    key_counts,
):
    n_dp = lax.axis_size("dp")
    factor = logit_scale / math.sqrt(HD)
    blocks, counts = key_blocks[0], key_counts[0]
    wq, wk, wv, wo = w_query[0], w_key[0], w_value[0], w_out[0]
    q, k, v, x = q_saved[0, 0], k_saved[0, 0], v_saved[0, 0], x_saved[0, 0]

    sent = pick(sent_forward[0, 0], encoded[0], grad_sent[0, 0], head_cotangent[0])
    ins = [crossed(sent, j) for j in range(3)]
    column_sets = column_parts(x, ins[0], norm_gain, n_dp)
    moved = exchanged(column_sets, "dp")
    soft, att = saved_attention(blocks, counts, factor, q, k, v, after=column_sets[:1])
    halves, token = half_relayed(ins[1], ins[2], after=[att, *moved[1:]])
    ins = ins + halves
    atts = exchanged([att] * n_dp, "dp")
    cols = stacked(moved, after=[token])
    cols = [cols] + [swapped(cols, "seq", j) for j in (1, 2)]

    grads = backward_attention(factor, ins, soft, wo, att, q, k, v, after=[cols[0], *atts[1:2]])
    ring = ring_gathered(grads, "dp")
    dx_near, dx_far = input_grads(grads, wq, wk, wv)
    dx_far = passed(dx_far, after=cols[1:])
    dx_came = swapped(dx_far, "seq", 1)
    cols = cols + [swapped(cols[1], "seq", 2)]
    mix_near, mix_far = forward_terms(
        blocks,
        counts,
        factor,
        ins,
        norm_gain,
        (wq, wk, wv, wo),
        after=[dx_far, *ring[1:2]],
    )
    mix_came = swapped(mix_far, "seq", 1)
    dx_sum = added(dx_near, dx_came, after=[mix_near])
    dx_last = swapped(dx_sum, "seq", 2)
    back_out, gain_part = back(dx_near, dx_came, dx_last, x, ins[0], norm_gain, after=[cols[3], *ring[2:3]])
    mix_sum = added(mix_near, mix_came, after=[back_out, *ring[3:4], *atts[3:]])
    mix_last = swapped(mix_sum, "seq", 2)

    gain_part = gain_added(gain_part, swapped(gain_part, "seq", 1), after=[mix_sum])
    gain_hop = swapped(gain_part, "seq", 2)
    grad_q, grad_k, grad_v = weight_grads(cols, ring, after=[gain_part])
    gain_part = gain_added(gain_part, gain_hop, after=[grad_q, mix_last])
    grad_out = out_weight_grads(cols, atts, after=[gain_part])
    gain_part = summed(gain_part, "dp")
    total = mix_near[0].astype(F32) + mix_came[0].astype(F32) + mix_last.astype(F32)
    forward_out = (ins[0][1].astype(F32) + total).astype(BF16)

    return (
        forward_out[None, None],
        back_out[None, None],
        grad_q[None],
        grad_k[None],
        grad_v[None],
        grad_out[None],
        gain_part,
    )


def solution(mesh):
    in_specs = (
        P("dp", "seq", None),
        P("pipe", "dp", "seq", None),
        P("dp", "seq", None),
        P("pipe", "dp", "seq", None),
        P("pipe", "dp", "seq", None),
        P("pipe", "dp", None, "seq"),
        P("pipe", "dp", None, "seq"),
        P("pipe", "dp", None, "seq"),
        P("pipe", None),
        P("pipe", "seq"),
        P("pipe", None, "seq"),
        P("pipe", None, "seq"),
        P("pipe", None, "seq"),
        P("pipe", "seq", None),
        P("dp", None, None),
        P("dp", None),
    )
    out_specs = (
        P("pipe", "dp", "seq", None),
        P("pipe", "dp", "seq", None),
        P("pipe", "dp", "seq"),
        P("pipe", "dp", "seq"),
        P("pipe", "dp", "seq"),
        P("pipe", "seq", "dp"),
        P("pipe", None),
    )
    return jax.shard_map(local, mesh=mesh, in_specs=in_specs, out_specs=out_specs, check_vma=False)
```
